256 devices in a mesh: row: 16 (over x_hi, y, core), col: 16 (over x_lo, z).
Axes of the slice: x: 4 (x_hi: 2, x_lo: 2; x = x_hi * 2 + x_lo), y: 4, z: 8, core: 2. Of those that a mesh axis runs over, the one named last changes fastest.
Arguments:
- pair: bfloat16 [2048, 2048, 128], P('row', 'col'), may hold values from -6 to 6
- ln_gain: float32 [128], replicated, may hold values from 0.5 to 1.5
- ln_bias: float32 [128], replicated, may hold values from -3 to 3
- w_proj: bfloat16 [128, 512], replicated, may hold values from -0.5 to 0.5
- w_gate: bfloat16 [128, 128], replicated, may hold values from -0.5 to 0.5
- out_gain: float32 [128], replicated, may hold values from 0.5 to 1.5
- out_bias: float32 [128], replicated, may hold values from -3 to 3
- w_out: bfloat16 [128, 128], replicated, may hold values from -0.5 to 0.5
Outputs:
- update: bfloat16 [2048, 2048, 128], P('row', 'col')
The draws below stay inside these ranges and needn't reach their ends.
All inputs are finite; a program needn't handle non-finite values.
Results may differ from the reference program's by a relative error of at most 0.0053.
Values may be sent and summed in bfloat16 or wider, within the bound.
No kernel may reach another device: no remote copies, remote signals or barrier semaphores. Data moves between devices by JAX's collectives and lax.ppermute only.
A program may use at most 128 MiB of HBM per device.

```python
import jax
import jax.numpy as jnp
from jax import lax

C = 128
HID = 128
TILE = 128
KW = 3
N = 2048
TJ = 128
N_COL = 16


def shard_levels(rng, extent, shards, least, top_value):
    factor_of, own = 1.0, jax.random.fold_in(rng, 6)
    for position, blocks in shards:
        steps = jnp.exp(jax.random.uniform(jax.random.fold_in(own, position), (blocks,), jnp.float32, least / len(shards), top_value / len(shards)))
        factor_of = factor_of * jnp.repeat(steps, extent[position] // blocks).reshape([-1 if axis == position else 1 for axis in range(len(extent))])
    return factor_of


def gaussian(key, dims, deviation, most, pieces=(), kind=jnp.bfloat16):
    values = jax.random.normal(key, dims, jnp.float32) * deviation
    if len(pieces) > 0:
        values = shard_levels(key, dims, pieces, -0.22, 0.18) * values
    return jnp.clip(values, min=-most, max=most).astype(kind)


def setup_inputs(seed: int = 0) -> dict:
    streams_of = jax.random.split(jax.random.key(seed), 9)
    return {
        "pair": gaussian(streams_of[0], (N, N, C), 1.0, 6.0, ((0, 16), (1, 16))),
        "ln_gain": jnp.clip(1.0 + 0.1 * jax.random.normal(streams_of[1], (C,), jnp.float32), 0.5, 1.5),
        "ln_bias": gaussian(streams_of[2], (C,), 0.5, 3.0, (), jnp.float32),
        "w_proj": gaussian(streams_of[3], (C, 4 * HID), C ** -0.5, 0.5),
        "w_gate": gaussian(streams_of[4], (C, C), C ** -0.5, 0.5),
        "out_gain": jnp.clip(1.0 + 0.1 * jax.random.normal(streams_of[5], (HID,), jnp.float32), 0.5, 1.5),
        "out_bias": gaussian(streams_of[6], (HID,), 0.5, 3.0, (), jnp.float32),
        "w_out": gaussian(streams_of[7], (HID, C), HID ** -0.5, 0.5),
    }


EPSILON = 1e-05

def normalize(values, scale_vec, shift_vec):
    average = lax.optimization_barrier(jnp.mean(values, axis=-1, keepdims=True))
    centred = values - average
    variance = lax.optimization_barrier(jnp.mean(centred * centred, axis=-1, keepdims=True))
    return centred * lax.rsqrt(variance + EPSILON) * scale_vec + shift_vec

def reference(pair, ln_gain, ln_bias, w_proj, w_gate, out_gain, out_bias, w_out):
    row_blocks = N // TILE

    def project_rows(block):
        start_row = (block * TILE).astype(jnp.int32)
        z_rows = lax.dynamic_slice_in_dim(pair, start_row, TILE, 0)
        normed = normalize(z_rows.astype(jnp.float32), ln_gain, ln_bias).astype(jnp.bfloat16)
        projected = jnp.dot(normed.reshape(-1, C), w_proj, preferred_element_type=jnp.float32)
        left_tile = (jax.nn.sigmoid(projected[:, :HID]) * projected[:, HID:2 * HID]).astype(jnp.bfloat16)
        right_tile = (jax.nn.sigmoid(projected[:, 2 * HID:3 * HID]) * projected[:, 3 * HID:]).astype(jnp.bfloat16)
        return (left_tile.reshape(TILE, N, HID), right_tile.reshape(TILE, N, HID))
    left_all, right_all = lax.map(project_rows, jnp.arange(row_blocks, dtype=jnp.int32))
    left_all = left_all.reshape(N, N, HID)
    right_all = right_all.reshape(N, N, HID)

    def out_block(block):
        row_block = (block // N_COL).astype(jnp.int32)
        col_block = (block % N_COL).astype(jnp.int32)
        row_start = (row_block * TILE).astype(jnp.int32)
        col_start = (col_block * TJ).astype(jnp.int32)
        zero_start = jnp.zeros((), jnp.int32)
        left_rows = lax.dynamic_slice_in_dim(left_all, row_start, TILE, 0)
        right_rows = lax.dynamic_slice_in_dim(right_all, col_start, TJ, 0)
        window = ((col_start + jnp.arange(KW * TJ, dtype=jnp.int32)) % N).astype(jnp.int32)
        left_win = jnp.take(left_rows, window, axis=1).astype(jnp.float32)
        right_win = jnp.take(right_rows, window, axis=1).astype(jnp.float32)
        contracted = jnp.einsum('ikh,jkh->ijh', left_win, right_win, precision=lax.Precision.HIGHEST)
        normed_out = normalize(contracted, out_gain, out_bias).astype(jnp.bfloat16)
        z_block = lax.dynamic_slice(pair, (row_start, col_start, zero_start), (TILE, TJ, C))
        normed = normalize(z_block.astype(jnp.float32), ln_gain, ln_bias).astype(jnp.bfloat16)
        gate = jax.nn.sigmoid(jnp.dot(normed.reshape(-1, C), w_gate, preferred_element_type=jnp.float32))
        projected_out = jnp.dot(normed_out.reshape(-1, HID), w_out, preferred_element_type=jnp.float32)
        return (gate * projected_out).astype(jnp.bfloat16).reshape(TILE, TJ, C)
    blocks = lax.map(out_block, jnp.arange(row_blocks * N_COL, dtype=jnp.int32))
    return blocks.reshape(row_blocks, N_COL, TILE, TJ, C).transpose(0, 2, 1, 3, 4).reshape(N, N, C)
```

```python
import functools

import jax
import jax.numpy as jnp
from jax import lax
from jax.experimental import pallas as pl
from jax.experimental.pallas import tpu as pltpu
from jax.sharding import PartitionSpec as P

EPSILON = 1e-05
F32, BF16 = jnp.float32, jnp.bfloat16
NT = (((1,), (1,)), ((), ()))
TN = (((0,), (0,)), ((), ()))
AXES = ("row", "col")
SUBS = ((0, 32), (32, 32), (64, 32), (96, 16))
RING = (112, 16)


def place(r, c):
    return (r % 16) * 16 + c % 16


def everyone(move):
    return [(place(r, c), place(*move(r, c))) for r in range(16) for c in range(16)]


def after_hops(c, hops):
    if hops >= 6:
        return (c - 8 + hops) % 16
    return c // 8 * 8 + (c + hops) % 8


def ring_pairs(hop):
    return [
        (place(r, after_hops(c, hop - 1)), place(r, after_hops(c, hop))) for r in range(16) for c in range(16)
    ]


def scatter_pairs(n):
    return [(place(c, c + d), place(c ^ (2 * n), c + d)) for c in range(16) for d in range(3)]


def shift_pairs():
    return everyone(lambda r, c: (r, c - 2) if (r - c) % 2 == 0 else (r ^ 1, c - 1))


def send(value, pairs):
    return lax.ppermute(value, AXES, pairs)


def sigmoid(x):
    return 0.5 * jnp.tanh(0.5 * x) + 0.5


def normed_rows(x, gain, bias):
    mean_of = jnp.full((128, 128), 1 / 128, BF16)
    centred = x.astype(F32) - jnp.dot(x, mean_of, preferred_element_type=F32)
    square = centred * centred
    high = square.astype(BF16)
    low = (square - high.astype(F32)).astype(BF16)
    variance = jnp.dot(high, mean_of, preferred_element_type=F32) + jnp.dot(
        low, mean_of, preferred_element_type=F32
    )
    return (centred * lax.rsqrt(variance + EPSILON) * gain + bias).astype(BF16)


def left_kernel(x_ref, gain_ref, bias_ref, wt_ref, wg_ref, left_ref, gate_ref, scratch):
    n = normed_rows(x_ref[...].reshape(16 * 128, 128), gain_ref[...], bias_ref[...])
    gate_ref[...] = sigmoid(jnp.dot(n, wg_ref[...], preferred_element_type=F32)).reshape(16, 128, 128)
    p = lax.dot_general(wt_ref[...], n, NT, preferred_element_type=F32)
    v = sigmoid(p[:128]) * p[128:]
    for i in range(16):
        scratch[i * 128 : (i + 1) * 128, :] = v[:, i * 128 : (i + 1) * 128]

    def turn(h, _):
        left_ref[h] = scratch[pl.ds(h, 16, stride=128), :].astype(BF16)
        return 0

    lax.fori_loop(0, 128, turn, 0, unroll=16)


def whole(a):
    return pl.BlockSpec(a.shape, lambda *_: (0,) * a.ndim)


def left_and_gate(pair, start, rows, gain, bias, wt, w_gate):
    first = start // 16
    return pl.pallas_call(
        left_kernel,
        out_shape=[
            jax.ShapeDtypeStruct((128, rows, 128), BF16),
            jax.ShapeDtypeStruct((rows, 128, 128), F32),
        ],
        grid=(rows // 16,),
        in_specs=[
            pl.BlockSpec((16, 128, 128), lambda i: (first + i, 0, 0)),
            whole(gain),
            whole(bias),
            whole(wt),
            whole(w_gate),
        ],
        out_specs=[
            pl.BlockSpec((128, 16, 128), lambda i: (0, i, 0)),
            pl.BlockSpec((16, 128, 128), lambda i: (i, 0, 0)),
        ],
        scratch_shapes=[pltpu.VMEM((16 * 128, 128), F32)],
        compiler_params=pltpu.CompilerParams(vmem_limit_bytes=48 << 20),
        cost_estimate=pl.CostEstimate(
            flops=rows * 128 * 128 * 2 * 768, bytes_accessed=rows * 128 * 128 * 8, transcendentals=rows * 128 * 256
        ),
    )(pair, gain, bias, wt, w_gate)


def right_kernel(x_ref, gain_ref, bias_ref, wt_ref, right_ref, scratch):
    d = pl.program_id(0)
    n = normed_rows(x_ref[...].reshape(16 * 128, 128), gain_ref[...], bias_ref[...])
    p = lax.dot_general(wt_ref[...], n, NT, preferred_element_type=F32)
    v = sigmoid(p[:64]) * p[64:]
    for j in range(16):
        scratch[j * 64 : (j + 1) * 64, :] = v[:, j * 128 : (j + 1) * 128]

    def turn(h, _):
        right_ref[h] = scratch[pl.ds(h, 16, stride=64), :].astype(BF16)
        return 0

    lax.fori_loop(0, 64, turn, 0, unroll=16)


def right_piece(pieces, gain, bias, wt):
    return pl.pallas_call(
        right_kernel,
        out_shape=jax.ShapeDtypeStruct((64, 16, 384), BF16),
        grid=(3,),
        in_specs=[pl.BlockSpec((16, 128, 128), lambda d: (d, 0, 0)), whole(gain), whole(bias), whole(wt)],
        out_specs=pl.BlockSpec((64, 16, 128), lambda d: (0, 0, d)),
        scratch_shapes=[pltpu.VMEM((16 * 64, 128), F32)],
        compiler_params=pltpu.CompilerParams(vmem_limit_bytes=32 << 20),
        cost_estimate=pl.CostEstimate(flops=48 * 128 * 128 * 2 * 384, bytes_accessed=3 << 20, transcendentals=48 * 128 * 64),
    )(pieces, gain, bias, wt)


STEP = 8


def final_kernel(place_ref, *refs, subs, aliased):
    count = len(subs)
    lefts = [refs[4 * s : 4 * s + 3] for s in range(count)]
    gates = [refs[4 * s + 3] for s in range(count)]
    rest = refs[4 * count :]
    rights, rest = rest[:16], rest[16:]
    gain_ref, bias_ref, w_ref = rest[:3]
    out_ref, scratch = rest[3 + aliased :]
    rows = sum(subs)
    step = pl.program_id(0)
    block, core = place_ref[0], place_ref[1]
    for half in range(2):
        which = core if half == 0 else 1 - core
        for t in range(STEP):
            left = jnp.concatenate(
                [jnp.concatenate([ref[which, t] for ref in sub], axis=-1) for sub in lefts], axis=0
            )
            right = jnp.concatenate([rights[2 * n + half][t] for n in range(8)], axis=0)
            h = which * 64 + step * STEP + t
            scratch[pl.ds(pl.multiple_of(h * rows, rows), rows), :] = lax.dot_general(
                left, right, NT, preferred_element_type=F32
            )

    @pl.when(step == 64 // STEP - 1)
    def _():
        base = 0
        for sub, gate_ref in zip(subs, gates):

            def some_rows(q, _, base=base, gate_ref=gate_ref):
                parts = []
                for e in range(8):
                    x = scratch[pl.ds(base + q * 8 + e, 128, stride=rows), :]
                    centred = x - jnp.mean(x, axis=0, keepdims=True)
                    variance = jnp.mean(centred * centred, axis=0, keepdims=True)
                    parts.append(
                        (centred * lax.rsqrt(variance + EPSILON) * gain_ref[...] + bias_ref[...]).astype(BF16)
                    )
                y = jnp.concatenate(parts, axis=1)
                out = lax.dot_general(y, w_ref[...], TN, preferred_element_type=F32)
                for e in range(8):
                    for n in range(8):
                        at = pl.ds(pl.multiple_of((block ^ n) * 16, 16), 16)
                        mine = out[e * 128 + n * 16 : e * 128 + n * 16 + 16]
                        out_ref[base + q * 8 + e, at, :] = (gate_ref[q * 8 + e, at, :] * mine).astype(BF16)
                return 0

            lax.fori_loop(0, sub // 8, some_rows, 0)
            base += sub


def final(where, groups, rights, gain, bias, w_out, update, block):
    subs = tuple(g[3].shape[0] for g in groups)
    rows = sum(subs)
    operands, specs = [], []
    for l0, l1, l2, gate in groups:
        for l in (l0, l1, l2):
            operands.append(l.reshape(2, 64, gate.shape[0], 128))
            specs.append(pl.BlockSpec((2, STEP, gate.shape[0], 128), lambda s, _: (0, s, 0, 0)))
        operands.append(gate)
        specs.append(whole(gate))
    operands += rights
    specs += [pl.BlockSpec((STEP, 16, 384), lambda s, _: (s, 0, 0))] * 16
    operands += [gain, bias, w_out]
    specs += [whole(gain), whole(bias), whole(w_out)]
    aliases = {}
    if update is not None:
        aliases = {1 + len(operands): 0}
        operands.append(update)
        specs.append(pl.BlockSpec(memory_space=pl.ANY))
    return pl.pallas_call(
        functools.partial(final_kernel, subs=subs, aliased=len(aliases)),
        out_shape=jax.ShapeDtypeStruct((128, 128, 128), BF16),
        grid_spec=pltpu.PrefetchScalarGridSpec(
            num_scalar_prefetch=1,
            grid=(64 // STEP,),
            in_specs=specs,
            out_specs=pl.BlockSpec((rows, 128, 128), lambda s, _: (block, 0, 0)),
            scratch_shapes=[pltpu.VMEM((128 * rows, 128), F32)],
        ),
        input_output_aliases=aliases,
        compiler_params=pltpu.CompilerParams(vmem_limit_bytes=56 << 20),
        cost_estimate=pl.CostEstimate(
            flops=rows * 128 * 128 * 2 * 512, bytes_accessed=(14 << 20) + rows * 128 * 128 * 12, transcendentals=0
        ),
    )(where, *operands)


def shards(pair, ln_gain, ln_bias, w_proj, w_gate, out_gain, out_bias, w_out):
    row, col = lax.axis_index("row"), lax.axis_index("col")
    core, chip = row % 2, row // 2
    gain, bias = ln_gain[None, :], ln_bias[None, :]

    pieces = [pair[:16]] + [send(pair[16 * n : 16 * n + 16], scatter_pairs(n)) for n in range(1, 8)]

    wt_left = w_proj[:, :256].T
    lefts = {}
    order = (RING,) + SUBS
    for start, rows in order:
        lefts[start] = left_and_gate(pair, start, rows, gain, bias, wt_left, w_gate)

    ring = [lefts[RING[0]][0]]
    for hop in range(1, 8):
        ring.append(send(ring[-1], ring_pairs(hop)))
    back = lambda r, c: (r, c - 1)
    once = {start: send(lefts[start][0], everyone(back)) for start, _ in SUBS}
    twice = {start: send(once[start], everyone(back)) for start, _ in SUBS}

    def piece_of(d):
        source = ((col - d) % 16) // 2
        picked = pieces[0]
        for n in range(1, 8):
            picked = jnp.where(chip ^ source == n, pieces[n], picked)
        return picked

    even = core == col % 2
    first = piece_of(0)
    second_or_third = jnp.where(even, piece_of(2), piece_of(1))
    shifted = send(second_or_third, shift_pairs())
    swap = lambda r, c: (r ^ 1, c)
    swapped_first = send(first, everyone(swap))
    swapped = send(shifted, everyone(swap))
    raw = jnp.concatenate(
        [
            jnp.where(even, first, swapped_first),
            jnp.where(even, swapped, shifted),
            jnp.where(even, shifted, swapped),
        ],
        axis=0,
    )
    half = [lax.dynamic_slice_in_dim(w_proj, 256 + 128 * v + 64 * core, 64, 1) for v in range(2)]
    mine = right_piece(raw, gain, bias, jnp.concatenate(half, axis=1).T)
    rights = []
    for n in range(8):
        got = mine if n == 0 else send(mine, everyone(lambda r, c, n=n: (r ^ (2 * n), c)))
        rights += [got, send(got, everyone(swap))]

    where = jnp.stack([chip ^ (col // 2), core]).astype(jnp.int32)
    out_g = jnp.broadcast_to(out_gain[:, None], (128, 128))
    out_b = jnp.broadcast_to(out_bias[:, None], (128, 128))

    def group(start):
        return (lefts[start][0], once[start], twice[start], lefts[start][1])

    update = None
    for block in range(3):
        update = final(where, [group(32 * block)], rights, out_g, out_b, w_out, update, block)
    last = (ring[0], ring[7], ring[6], lefts[RING[0]][1])
    return final(where, [group(96), last], rights, out_g, out_b, w_out, update, 3)


def solution(mesh):
    in_specs = (P("row", "col", None), P(), P(), P(), P(), P(), P(), P())
    out_specs = P("row", "col", None)
    return jax.shard_map(shards, mesh=mesh, in_specs=in_specs, out_specs=out_specs, check_vma=False)
```

```python
import functools

import jax
import jax.numpy as jnp
from jax import lax
from jax.experimental import pallas as pl
from jax.experimental.pallas import tpu as pltpu
from jax.sharding import PartitionSpec as P

EPSILON = 1e-05
F32, BF16 = jnp.float32, jnp.bfloat16
NT = (((1,), (1,)), ((), ()))
TN = (((0,), (0,)), ((), ()))
AXES = ("row", "col")
BIG, SMALL, RING = (0, 64), (64, 32), (96, 32)
EARLY = (64,)


def place(r, c):
    return (r % 16) * 16 + c % 16


def everyone(move):
    return [(place(r, c), place(*move(r, c))) for r in range(16) for c in range(16)]


def after_hops(c, hops):
    if hops >= 6:
        return (c - 8 + hops) % 16
    return c // 8 * 8 + (c + hops) % 8


def ring_pairs(hop):
    return [
        (place(r, after_hops(c, hop - 1)), place(r, after_hops(c, hop))) for r in range(16) for c in range(16)
    ]


def scatter_pairs(n):
    return [(place(c, c + d), place(c ^ (2 * n), c + d)) for c in range(16) for d in range(3)]


def shift_pairs():
    return everyone(lambda r, c: (r, c - 2) if (r - c) % 2 == 0 else (r ^ 1, c - 1))


def swap_first(r, c):
    return (r, c + 8) if c % 8 == 0 else (r, c)


def straight(r, c):
    return (r, c + 7) if c % 8 == 0 else (r, c - 1)


def back(r, c):
    return (r, c - 1)


def swap(r, c):
    return (r ^ 1, c)


def one_back(value, start):
    if start in EARLY:
        return send(send(value, everyone(swap_first)), everyone(straight))
    return send(value, everyone(back))


def after(value, *others):
    return lax.optimization_barrier((value,) + others)[0]


def send(value, pairs):
    return lax.ppermute(value, AXES, pairs)


def sigmoid(x):
    return 0.5 * jnp.tanh(0.5 * x) + 0.5


def normed_rows(x, gain, bias):
    mean_of = jnp.full((128, 128), 1 / 128, BF16)
    centred = x.astype(F32) - jnp.dot(x, mean_of, preferred_element_type=F32)
    square = centred * centred
    high = square.astype(BF16)
    low = (square - high.astype(F32)).astype(BF16)
    variance = jnp.dot(high, mean_of, preferred_element_type=F32) + jnp.dot(
        low, mean_of, preferred_element_type=F32
    )
    return (centred * lax.rsqrt(variance + EPSILON) * gain + bias).astype(BF16)


def left_kernel(x_ref, gain_ref, bias_ref, wt_ref, wg_ref, left_ref, gate_ref, scratch):
    n = normed_rows(x_ref[...].reshape(16 * 128, 128), gain_ref[...], bias_ref[...])
    gate_ref[...] = sigmoid(jnp.dot(n, wg_ref[...], preferred_element_type=F32)).reshape(16, 128, 128)
    p = lax.dot_general(wt_ref[...], n, NT, preferred_element_type=F32)
    v = sigmoid(p[:128]) * p[128:]
    for i in range(16):
        scratch[i * 128 : (i + 1) * 128, :] = v[:, i * 128 : (i + 1) * 128]

    def turn(h, _):
        left_ref[h] = scratch[pl.ds(h, 16, stride=128), :].astype(BF16)
        return 0

    lax.fori_loop(0, 128, turn, 0, unroll=16)


def whole(a):
    return pl.BlockSpec(a.shape, lambda *_: (0,) * a.ndim)


def left_and_gate(pair, start, rows, gain, bias, wt, w_gate):
    first = start // 16
    return pl.pallas_call(
        left_kernel,
        out_shape=[
            jax.ShapeDtypeStruct((128, rows, 128), BF16),
            jax.ShapeDtypeStruct((rows, 128, 128), F32),
        ],
        grid=(rows // 16,),
        in_specs=[
            pl.BlockSpec((16, 128, 128), lambda i: (first + i, 0, 0)),
            whole(gain),
            whole(bias),
            whole(wt),
            whole(w_gate),
        ],
        out_specs=[
            pl.BlockSpec((128, 16, 128), lambda i: (0, i, 0)),
            pl.BlockSpec((16, 128, 128), lambda i: (i, 0, 0)),
        ],
        scratch_shapes=[pltpu.VMEM((16 * 128, 128), F32)],
        compiler_params=pltpu.CompilerParams(vmem_limit_bytes=48 << 20),
        cost_estimate=pl.CostEstimate(
            flops=rows * 128 * 128 * 2 * 768, bytes_accessed=rows * 128 * 128 * 8, transcendentals=rows * 128 * 256
        ),
    )(pair, gain, bias, wt, w_gate)


def right_kernel(x_ref, gain_ref, bias_ref, wt_ref, right_ref, scratch):
    d = pl.program_id(0)
    n = normed_rows(x_ref[...].reshape(16 * 128, 128), gain_ref[...], bias_ref[...])
    p = lax.dot_general(wt_ref[...], n, NT, preferred_element_type=F32)
    v = sigmoid(p[:64]) * p[64:]
    for j in range(16):
        scratch[j * 64 : (j + 1) * 64, :] = v[:, j * 128 : (j + 1) * 128]

    def turn(h, _):
        right_ref[h] = scratch[pl.ds(h, 16, stride=64), :].astype(BF16)
        return 0

    lax.fori_loop(0, 64, turn, 0, unroll=16)


def right_piece(pieces, gain, bias, wt):
    return pl.pallas_call(
        right_kernel,
        out_shape=jax.ShapeDtypeStruct((64, 16, 384), BF16),
        grid=(3,),
        in_specs=[pl.BlockSpec((16, 128, 128), lambda d: (d, 0, 0)), whole(gain), whole(bias), whole(wt)],
        out_specs=pl.BlockSpec((64, 16, 128), lambda d: (0, 0, d)),
        scratch_shapes=[pltpu.VMEM((16 * 64, 128), F32)],
        compiler_params=pltpu.CompilerParams(vmem_limit_bytes=32 << 20),
        cost_estimate=pl.CostEstimate(flops=48 * 128 * 128 * 2 * 384, bytes_accessed=3 << 20, transcendentals=48 * 128 * 64),
    )(pieces, gain, bias, wt)


STEP = 8


def final_kernel(place_ref, *refs, subs, aliased):
    count = len(subs)
    lefts = [refs[4 * s : 4 * s + 3] for s in range(count)]
    gates = [refs[4 * s + 3] for s in range(count)]
    rest = refs[4 * count :]
    rights, rest = rest[:16], rest[16:]
    gain_ref, bias_ref, w_ref = rest[:3]
    out_ref, scratch = rest[3 + aliased :]
    rows = sum(subs)
    step = pl.program_id(0)
    block, core = place_ref[0], place_ref[1]
    for half in range(2):
        which = core if half == 0 else 1 - core
        for t in range(STEP):
            left = jnp.concatenate(
                [jnp.concatenate([ref[which, t] for ref in sub], axis=-1) for sub in lefts], axis=0
            )
            right = jnp.concatenate([rights[2 * n + half][t] for n in range(8)], axis=0)
            h = which * 64 + step * STEP + t
            scratch[pl.ds(pl.multiple_of(h * rows, rows), rows), :] = lax.dot_general(
                left, right, NT, preferred_element_type=F32
            )

    @pl.when(step == 64 // STEP - 1)
    def _():
        base = 0
        for sub, gate_ref in zip(subs, gates):

            def some_rows(q, _, base=base, gate_ref=gate_ref):
                parts = []
                for e in range(8):
                    x = scratch[pl.ds(base + q * 8 + e, 128, stride=rows), :]
                    centred = x - jnp.mean(x, axis=0, keepdims=True)
                    variance = jnp.mean(centred * centred, axis=0, keepdims=True)
                    parts.append(
                        (centred * lax.rsqrt(variance + EPSILON) * gain_ref[...] + bias_ref[...]).astype(BF16)
                    )
                y = jnp.concatenate(parts, axis=1)
                out = lax.dot_general(y, w_ref[...], TN, preferred_element_type=F32)
                for e in range(8):
                    for n in range(8):
                        at = pl.ds(pl.multiple_of((block ^ n) * 16, 16), 16)
                        mine = out[e * 128 + n * 16 : e * 128 + n * 16 + 16]
                        out_ref[base + q * 8 + e, at, :] = (gate_ref[q * 8 + e, at, :] * mine).astype(BF16)
                return 0

            lax.fori_loop(0, sub // 8, some_rows, 0)
            base += sub


def final(where, groups, rights, gain, bias, w_out, update, block):
    subs = tuple(g[3].shape[0] for g in groups)
    rows = sum(subs)
    operands, specs = [], []
    for l0, l1, l2, gate in groups:
        for l in (l0, l1, l2):
            operands.append(l.reshape(2, 64, gate.shape[0], 128))
            specs.append(pl.BlockSpec((2, STEP, gate.shape[0], 128), lambda s, _: (0, s, 0, 0)))
        operands.append(gate)
        specs.append(whole(gate))
    operands += rights
    specs += [pl.BlockSpec((STEP, 16, 384), lambda s, _: (s, 0, 0))] * 16
    operands += [gain, bias, w_out]
    specs += [whole(gain), whole(bias), whole(w_out)]
    aliases = {}
    if update is not None:
        aliases = {1 + len(operands): 0}
        operands.append(update)
        specs.append(pl.BlockSpec(memory_space=pl.ANY))
    return pl.pallas_call(
        functools.partial(final_kernel, subs=subs, aliased=len(aliases)),
        out_shape=jax.ShapeDtypeStruct((128, 128, 128), BF16),
        grid_spec=pltpu.PrefetchScalarGridSpec(
            num_scalar_prefetch=1,
            grid=(64 // STEP,),
            in_specs=specs,
            out_specs=pl.BlockSpec((rows, 128, 128), lambda s, _: (block, 0, 0)),
            scratch_shapes=[pltpu.VMEM((128 * rows, 128), F32)],
        ),
        input_output_aliases=aliases,
        compiler_params=pltpu.CompilerParams(vmem_limit_bytes=56 << 20),
        cost_estimate=pl.CostEstimate(
            flops=rows * 128 * 128 * 2 * 512, bytes_accessed=(14 << 20) + rows * 128 * 128 * 12, transcendentals=0
        ),
    )(where, *operands)


def shards(pair, ln_gain, ln_bias, w_proj, w_gate, out_gain, out_bias, w_out):
    row, col = lax.axis_index("row"), lax.axis_index("col")
    core, chip = row % 2, row // 2
    gain, bias = ln_gain[None, :], ln_bias[None, :]

    wt_left = w_proj[:, :256].T

    def left_of(part, source):
        return left_and_gate(source, *part, gain, bias, wt_left, w_gate)

    pieces = {0: pair[:16]}
    for n in (7, 6, 5):
        pieces[n] = send(pair[16 * n : 16 * n + 16], scatter_pairs(n))
    big, big_gate = left_of(BIG, pair)
    big_once = one_back(big, BIG[0])
    whirl, whirl_gate = left_of(RING, pair)
    ring = [whirl]
    ring.append(send(ring[-1], ring_pairs(1)))
    raw_pair = after(pair, whirl, big)
    for n in (4, 3, 1, 2):
        pieces[n] = send(raw_pair[16 * n : 16 * n + 16], scatter_pairs(n))

    def piece_of(d):
        source = ((col - d) % 16) // 2
        picked = pieces[0]
        for n in range(1, 8):
            picked = jnp.where(chip ^ source == n, pieces[n], picked)
        return picked

    even = core == col % 2
    first = piece_of(0)
    second_or_third = jnp.where(even, piece_of(2), piece_of(1))
    second_or_third = after(second_or_third, ring[1])
    shifted = send(second_or_third, shift_pairs())
    ring.append(send(after(ring[1], second_or_third), ring_pairs(2)))
    small, small_gate = left_of(SMALL, after(pair, second_or_third))
    shifted = after(shifted, big_once, ring[2], small)
    big_twice = one_back(after(big_once, shifted), BIG[0])
    ring.append(send(after(ring[2], shifted), ring_pairs(3)))
    swapped_first = send(first, everyone(swap))
    swapped = send(shifted, everyone(swap))
    raw = jnp.concatenate(
        [
            jnp.where(even, first, swapped_first),
            jnp.where(even, swapped, shifted),
            jnp.where(even, shifted, swapped),
        ],
        axis=0,
    )
    half = [lax.dynamic_slice_in_dim(w_proj, 256 + 128 * v + 64 * core, 64, 1) for v in range(2)]
    mine = right_piece(raw, gain, bias, jnp.concatenate(half, axis=1).T)
    got = {0: mine}

    def exchange(value, n):
        return send(value, everyone(lambda r, c: (r ^ (2 * n), c)))

    for n in (4, 1, 3):
        got[n] = exchange(mine, n)
    small_once = one_back(after(small, mine), SMALL[0])
    stage = after(got[4], got[1], got[3], ring[3], big_twice)
    got[5], got[7] = exchange(stage, 1), exchange(stage, 3)
    got[2] = exchange(after(mine, stage), 2)
    ring.append(send(after(ring[3], stage), ring_pairs(4)))
    stage = after(got[4], got[5], got[7], ring[4], got[2])
    got[6] = exchange(stage, 2)
    ring.append(send(after(ring[4], stage), ring_pairs(5)))
    small_twice = one_back(after(small_once, got[2]), SMALL[0])
    ring.append(send(after(ring[5], got[2]), ring_pairs(6)))
    ring.append(send(after(ring[6], got[6]), ring_pairs(7)))
    rights = []
    for n in range(8):
        rights += [got[n], send(got[n], everyone(swap))]

    where = jnp.stack([chip ^ (col // 2), core]).astype(jnp.int32)
    out_g = jnp.broadcast_to(out_gain[:, None], (128, 128))
    out_b = jnp.broadcast_to(out_bias[:, None], (128, 128))

    groups = [
        (big, big_once, big_twice, big_gate),
        (small, small_once, small_twice, small_gate),
        (whirl, ring[7], ring[6], whirl_gate),
    ]
    return final(where, groups, rights, out_g, out_b, w_out, None, 0)


def solution(mesh):
    in_specs = (P("row", "col", None), P(), P(), P(), P(), P(), P(), P())
    out_specs = P("row", "col", None)
    return jax.shard_map(shards, mesh=mesh, in_specs=in_specs, out_specs=out_specs, check_vma=False)
```

```python
import functools

import jax
import jax.numpy as jnp
from jax import lax
from jax.experimental import pallas as pl
from jax.experimental.pallas import tpu as pltpu
from jax.sharding import PartitionSpec as P

EPSILON = 1e-05
F32, BF16 = jnp.float32, jnp.bfloat16
NT = (((1,), (1,)), ((), ()))
TN = (((0,), (0,)), ((), ()))
AXES = ("row", "col")
ROWS = 32


def place(r, c):
    return (r % 16) * 16 + c % 16


def everyone(move):
    return [(place(r, c), place(*move(r, c))) for r in range(16) for c in range(16)]


def side(row):
    return row % 16 // 8


def scatter_pairs(a):
    return [(place(c, c + d), place(c ^ (2 * a), c + d)) for c in range(16) for d in range(3)]


def across_pairs(third):
    pairs = []
    for r in range(16):
        for c in range(16):
            even = (r - c) % 2 == 0
            d = 2 if third else 0 if even else 1
            if (even or not third) and side(r) == side(c - d):
                pairs.append((place(r, c), place(r ^ 8, c)))
    return pairs


def shift_pairs():
    return everyone(lambda r, c: (r, c - 2) if (r - c) % 2 == 0 else (r ^ 1, c - 1))


def back(r, c):
    return (r, c - 1)


def swap(r, c):
    return (r ^ 1, c)


def after(value, *others):
    return lax.optimization_barrier((value,) + others)[0]


def send(value, pairs):
    return lax.ppermute(value, AXES, pairs)


def sigmoid(x):
    return 0.5 * jnp.tanh(0.5 * x) + 0.5


def normed_rows(x, gain, bias):
    mean_of = jnp.full((128, 128), 1 / 128, BF16)
    centred = x.astype(F32) - jnp.dot(x, mean_of, preferred_element_type=F32)
    square = centred * centred
    high = square.astype(BF16)
    low = (square - high.astype(F32)).astype(BF16)
    variance = jnp.dot(high, mean_of, preferred_element_type=F32) + jnp.dot(
        low, mean_of, preferred_element_type=F32
    )
    return (centred * lax.rsqrt(variance + EPSILON) * gain + bias).astype(BF16)


def left_kernel(x_ref, gain_ref, bias_ref, wt_ref, wg_ref, left_ref, gate_ref, scratch):
    n = normed_rows(x_ref[...].reshape(16 * 128, 128), gain_ref[...], bias_ref[...])
    gate_ref[...] = sigmoid(jnp.dot(n, wg_ref[...], preferred_element_type=F32)).reshape(16, 128, 128)
    p = lax.dot_general(wt_ref[...], n, NT, preferred_element_type=F32)
    v = sigmoid(p[:128]) * p[128:]
    for i in range(16):
        scratch[i * 128 : (i + 1) * 128, :] = v[:, i * 128 : (i + 1) * 128]

    def turn(h, _):
        left_ref[h] = scratch[pl.ds(h, 16, stride=128), :].astype(BF16)
        return 0

    lax.fori_loop(0, 128, turn, 0, unroll=16)


def whole(a):
    return pl.BlockSpec(a.shape, lambda *_: (0,) * a.ndim)


def left_and_gate(pair, start, rows, gain, bias, wt, w_gate):
    first = start // 16
    return pl.pallas_call(
        left_kernel,
        out_shape=[
            jax.ShapeDtypeStruct((128, rows, 128), BF16),
            jax.ShapeDtypeStruct((rows, 128, 128), F32),
        ],
        grid=(rows // 16,),
        in_specs=[
            pl.BlockSpec((16, 128, 128), lambda i: (first + i, 0, 0)),
            whole(gain),
            whole(bias),
            whole(wt),
            whole(w_gate),
        ],
        out_specs=[
            pl.BlockSpec((128, 16, 128), lambda i: (0, i, 0)),
            pl.BlockSpec((16, 128, 128), lambda i: (i, 0, 0)),
        ],
        scratch_shapes=[pltpu.VMEM((16 * 128, 128), F32)],
        compiler_params=pltpu.CompilerParams(vmem_limit_bytes=48 << 20),
        cost_estimate=pl.CostEstimate(
            flops=rows * 128 * 128 * 2 * 768, bytes_accessed=rows * 128 * 128 * 8, transcendentals=rows * 128 * 256
        ),
    )(pair, gain, bias, wt, w_gate)


def right_kernel(x_ref, gain_ref, bias_ref, wt_ref, right_ref, scratch):
    d = pl.program_id(0)
    n = normed_rows(x_ref[...].reshape(16 * 128, 128), gain_ref[...], bias_ref[...])
    p = lax.dot_general(wt_ref[...], n, NT, preferred_element_type=F32)
    v = sigmoid(p[:64]) * p[64:]
    for j in range(16):
        scratch[j * 64 : (j + 1) * 64, :] = v[:, j * 128 : (j + 1) * 128]

    def turn(h, _):
        right_ref[h] = scratch[pl.ds(h, 16, stride=64), :].astype(BF16)
        return 0

    lax.fori_loop(0, 64, turn, 0, unroll=16)


def right_piece(pieces, gain, bias, wt):
    return pl.pallas_call(
        right_kernel,
        out_shape=jax.ShapeDtypeStruct((64, 16, 384), BF16),
        grid=(3,),
        in_specs=[pl.BlockSpec((16, 128, 128), lambda d: (d, 0, 0)), whole(gain), whole(bias), whole(wt)],
        out_specs=pl.BlockSpec((64, 16, 128), lambda d: (0, 0, d)),
        scratch_shapes=[pltpu.VMEM((16 * 64, 128), F32)],
        compiler_params=pltpu.CompilerParams(vmem_limit_bytes=32 << 20),
        cost_estimate=pl.CostEstimate(flops=48 * 128 * 128 * 2 * 384, bytes_accessed=3 << 20, transcendentals=48 * 128 * 64),
    )(pieces, gain, bias, wt)


STEP = 8


def final_kernel(place_ref, *refs, subs, aliased):
    count = len(subs)
    lefts = [refs[4 * s : 4 * s + 3] for s in range(count)]
    gates = [refs[4 * s + 3] for s in range(count)]
    rest = refs[4 * count :]
    rights, rest = rest[:16], rest[16:]
    gain_ref, bias_ref, w_ref = rest[:3]
    out_ref, scratch = rest[3 + aliased :]
    rows = sum(subs)
    step = pl.program_id(0)
    block, core = place_ref[0], place_ref[1]
    for half in range(2):
        which = core if half == 0 else 1 - core
        for t in range(STEP):
            left = jnp.concatenate(
                [jnp.concatenate([ref[which, t] for ref in sub], axis=-1) for sub in lefts], axis=0
            )
            right = jnp.concatenate([rights[2 * n + half][t] for n in range(8)], axis=0)
            h = which * 64 + step * STEP + t
            scratch[pl.ds(pl.multiple_of(h * rows, rows), rows), :] = lax.dot_general(
                left, right, NT, preferred_element_type=F32
            )

    @pl.when(step == 64 // STEP - 1)
    def _():
        base = 0
        for sub, gate_ref in zip(subs, gates):

            def some_rows(q, _, base=base, gate_ref=gate_ref):
                parts = []
                for e in range(8):
                    x = scratch[pl.ds(base + q * 8 + e, 128, stride=rows), :]
                    centred = x - jnp.mean(x, axis=0, keepdims=True)
                    variance = jnp.mean(centred * centred, axis=0, keepdims=True)
                    parts.append(
                        (centred * lax.rsqrt(variance + EPSILON) * gain_ref[...] + bias_ref[...]).astype(BF16)
                    )
                y = jnp.concatenate(parts, axis=1)
                out = lax.dot_general(y, w_ref[...], TN, preferred_element_type=F32)
                for e in range(8):
                    for n in range(8):
                        chip = block ^ n
                        at = pl.ds(pl.multiple_of(chip % 4 * 32 + chip // 4 * 16, 16), 16)
                        mine = out[e * 128 + n * 16 : e * 128 + n * 16 + 16]
                        out_ref[base + q * 8 + e, at, :] = (gate_ref[q * 8 + e, at, :] * mine).astype(BF16)
                return 0

            lax.fori_loop(0, sub // 8, some_rows, 0)
            base += sub


def final(where, groups, rights, gain, bias, w_out, update, block):
    subs = tuple(g[3].shape[0] for g in groups)
    rows = sum(subs)
    operands, specs = [], []
    for l0, l1, l2, gate in groups:
        for l in (l0, l1, l2):
            operands.append(l.reshape(2, 64, gate.shape[0], 128))
            specs.append(pl.BlockSpec((2, STEP, gate.shape[0], 128), lambda s, _: (0, s, 0, 0)))
        operands.append(gate)
        specs.append(whole(gate))
    operands += rights
    specs += [pl.BlockSpec((STEP, 16, 384), lambda s, _: (s, 0, 0))] * 16
    operands += [gain, bias, w_out]
    specs += [whole(gain), whole(bias), whole(w_out)]
    aliases = {}
    if update is not None:
        aliases = {1 + len(operands): 0}
        operands.append(update)
        specs.append(pl.BlockSpec(memory_space=pl.ANY))
    return pl.pallas_call(
        functools.partial(final_kernel, subs=subs, aliased=len(aliases)),
        out_shape=jax.ShapeDtypeStruct((128, 128, 128), BF16),
        grid_spec=pltpu.PrefetchScalarGridSpec(
            num_scalar_prefetch=1,
            grid=(64 // STEP,),
            in_specs=specs,
            out_specs=pl.BlockSpec((rows, 128, 128), lambda s, _: (block, 0, 0)),
            scratch_shapes=[pltpu.VMEM((128 * rows, 128), F32)],
        ),
        input_output_aliases=aliases,
        compiler_params=pltpu.CompilerParams(vmem_limit_bytes=56 << 20),
        cost_estimate=pl.CostEstimate(
            flops=rows * 128 * 128 * 2 * 512, bytes_accessed=(14 << 20) + rows * 128 * 128 * 12, transcendentals=0
        ),
    )(where, *operands)


def shards(pair, ln_gain, ln_bias, w_proj, w_gate, out_gain, out_bias, w_out):
    row, col = lax.axis_index("row"), lax.axis_index("col")
    core, chip = row % 2, row // 2
    gain, bias = ln_gain[None, :], ln_bias[None, :]

    wt_left = w_proj[:, :256].T

    def left_of(q, source):
        return left_and_gate(source, ROWS * q, ROWS, gain, bias, wt_left, w_gate)

    def one_back(value):
        return send(value, everyone(back))

    quarters = [pair[:32]] + [send(pair[32 * a : 32 * a + 32], scatter_pairs(a)) for a in (1, 2, 3)]
    lefts = [left_of(q, pair) for q in range(3)]
    once = [one_back(lefts[0][0]), one_back(lefts[1][0])]
    once.append(one_back(after(lefts[2][0], once[0])))
    quarters[1] = after(quarters[1], lefts[1][0])
    even = core == col % 2
    y, x_side = chip % 4, chip // 4

    def quarter_of(d):
        away = y ^ ((col - d) % 16 // 2 % 4)
        picked = quarters[0]
        for a in range(1, 4):
            picked = jnp.where(away == a, quarters[a], picked)
        return picked

    one = jnp.where(even, quarter_of(0), quarter_of(1))
    two = quarter_of(2)
    one_across = send(one[16:], across_pairs(False))
    two_across = send(two[16:], across_pairs(True))
    d_one = jnp.where(even, 0, 1)
    one = jnp.where(x_side == (col - d_one) % 16 // 8, one[:16], one_across)
    two = jnp.where(x_side == (col - 2) % 16 // 8, two[:16], two_across)
    moving = jnp.where(even, two, one)
    shifted = send(moving, shift_pairs())
    swapped_one = send(one, everyone(swap))
    lefts.append(left_of(3, after(pair, moving)))
    once.append(one_back(lefts[3][0]))
    shifted = after(shifted, once[1], once[2], swapped_one, lefts[3][0])
    twice = [one_back(after(once[0], shifted))]
    swapped = send(shifted, everyone(swap))
    first, swapped_first = one, swapped_one
    raw = jnp.concatenate(
        [
            jnp.where(even, first, swapped_first),
            jnp.where(even, swapped, shifted),
            jnp.where(even, shifted, swapped),
        ],
        axis=0,
    )
    half = [lax.dynamic_slice_in_dim(w_proj, 256 + 128 * v + 64 * core, 64, 1) for v in range(2)]
    mine = right_piece(raw, gain, bias, jnp.concatenate(half, axis=1).T)
    got = {0: mine}

    def exchange(value, n):
        return send(value, everyone(lambda r, c: (r ^ (2 * n), c)))

    for n in (4, 1, 3):
        got[n] = exchange(mine, n)
    twice.append(one_back(after(once[1], mine)))
    stage = after(got[4], got[1], got[3], once[3])
    got[5], got[7] = exchange(stage, 1), exchange(stage, 3)
    got[2] = exchange(after(mine, stage), 2)
    twice.append(one_back(after(once[2], stage)))
    stage = after(got[4], got[5], got[7], got[2], twice[0])
    got[6] = exchange(stage, 2)
    twice.append(one_back(after(once[3], stage)))
    rights = []
    for n in range(8):
        rights += [got[n], send(got[n], everyone(swap))]

    where = jnp.stack([chip ^ (col // 2), core]).astype(jnp.int32)
    out_g = jnp.broadcast_to(out_gain[:, None], (128, 128))
    out_b = jnp.broadcast_to(out_bias[:, None], (128, 128))

    groups = [(lefts[q][0], once[q], twice[q], lefts[q][1]) for q in range(4)]
    update = final(after(where, twice[2]), groups[:2], rights, out_g, out_b, w_out, None, 0)
    return final(where, groups[2:], rights, out_g, out_b, w_out, update, 1)


def solution(mesh):
    in_specs = (P("row", "col", None), P(), P(), P(), P(), P(), P(), P())
    out_specs = P("row", "col", None)
    return jax.shard_map(shards, mesh=mesh, in_specs=in_specs, out_specs=out_specs, check_vma=False)
```

```python
import functools

import jax
import jax.numpy as jnp
from jax import lax
from jax.experimental import pallas as pl
from jax.experimental.pallas import tpu as pltpu
from jax.sharding import PartitionSpec as P

EPSILON = 1e-05
F32, BF16 = jnp.float32, jnp.bfloat16
NT = (((1,), (1,)), ((), ()))
TN = (((0,), (0,)), ((), ()))
AXES = ("row", "col")
BIG, SMALL = (0, 80), (80, 48)


def place(r, c):
    return (r % 16) * 16 + c % 16


def everyone(move):
    return [(place(r, c), place(*move(r, c))) for r in range(16) for c in range(16)]


def side(row):
    return row % 16 // 8


def scatter_pairs(a):
    return [(place(c, c + d), place(c ^ (2 * a), c + d)) for c in range(16) for d in range(3)]


def across_pairs(third):
    pairs = []
    for r in range(16):
        for c in range(16):
            even = (r - c) % 2 == 0
            d = 2 if third else 0 if even else 1
            if (even or not third) and side(r) == side(c - d):
                pairs.append((place(r, c), place(r ^ 8, c)))
    return pairs


def shift_pairs():
    return everyone(lambda r, c: (r, c - 2) if (r - c) % 2 == 0 else (r ^ 1, c - 1))


def back(r, c):
    return (r, c - 1)


def swap(r, c):
    return (r ^ 1, c)


def after(value, *others):
    return lax.optimization_barrier((value,) + others)[0]


def send(value, pairs):
    return lax.ppermute(value, AXES, pairs)


def sigmoid(x):
    return 0.5 * jnp.tanh(0.5 * x) + 0.5


def normed_rows(x, gain, bias):
    mean_of = jnp.full((128, 128), 1 / 128, BF16)
    centred = x.astype(F32) - jnp.dot(x, mean_of, preferred_element_type=F32)
    square = centred * centred
    high = square.astype(BF16)
    low = (square - high.astype(F32)).astype(BF16)
    variance = jnp.dot(high, mean_of, preferred_element_type=F32) + jnp.dot(
        low, mean_of, preferred_element_type=F32
    )
    return (centred * lax.rsqrt(variance + EPSILON) * gain + bias).astype(BF16)


def left_kernel(x_ref, gain_ref, bias_ref, wt_ref, wg_ref, left_ref, gate_ref, scratch):
    n = normed_rows(x_ref[...].reshape(16 * 128, 128), gain_ref[...], bias_ref[...])
    gate_ref[...] = sigmoid(jnp.dot(n, wg_ref[...], preferred_element_type=F32)).reshape(16, 128, 128)
    p = lax.dot_general(wt_ref[...], n, NT, preferred_element_type=F32)
    v = sigmoid(p[:128]) * p[128:]
    for i in range(16):
        scratch[i * 128 : (i + 1) * 128, :] = v[:, i * 128 : (i + 1) * 128]

    def turn(h, _):
        left_ref[h] = scratch[pl.ds(h, 16, stride=128), :].astype(BF16)
        return 0

    lax.fori_loop(0, 128, turn, 0, unroll=16)


def whole(a):
    return pl.BlockSpec(a.shape, lambda *_: (0,) * a.ndim)


def left_and_gate(pair, start, rows, gain, bias, wt, w_gate):
    first = start // 16
    return pl.pallas_call(
        left_kernel,
        out_shape=[
            jax.ShapeDtypeStruct((128, rows, 128), BF16),
            jax.ShapeDtypeStruct((rows, 128, 128), F32),
        ],
        grid=(rows // 16,),
        in_specs=[
            pl.BlockSpec((16, 128, 128), lambda i: (first + i, 0, 0)),
            whole(gain),
            whole(bias),
            whole(wt),
            whole(w_gate),
        ],
        out_specs=[
            pl.BlockSpec((128, 16, 128), lambda i: (0, i, 0)),
            pl.BlockSpec((16, 128, 128), lambda i: (i, 0, 0)),
        ],
        scratch_shapes=[pltpu.VMEM((16 * 128, 128), F32)],
        compiler_params=pltpu.CompilerParams(vmem_limit_bytes=48 << 20),
        cost_estimate=pl.CostEstimate(
            flops=rows * 128 * 128 * 2 * 768, bytes_accessed=rows * 128 * 128 * 8, transcendentals=rows * 128 * 256
        ),
    )(pair, gain, bias, wt, w_gate)


def right_kernel(x_ref, gain_ref, bias_ref, wt_ref, right_ref, scratch):
    d = pl.program_id(0)
    n = normed_rows(x_ref[...].reshape(16 * 128, 128), gain_ref[...], bias_ref[...])
    p = lax.dot_general(wt_ref[...], n, NT, preferred_element_type=F32)
    v = sigmoid(p[:64]) * p[64:]
    for j in range(16):
        scratch[j * 64 : (j + 1) * 64, :] = v[:, j * 128 : (j + 1) * 128]

    def turn(h, _):
        right_ref[h] = scratch[pl.ds(h, 16, stride=64), :].astype(BF16)
        return 0

    lax.fori_loop(0, 64, turn, 0, unroll=16)


def right_piece(pieces, gain, bias, wt):
    return pl.pallas_call(
        right_kernel,
        out_shape=jax.ShapeDtypeStruct((64, 16, 384), BF16),
        grid=(3,),
        in_specs=[pl.BlockSpec((16, 128, 128), lambda d: (d, 0, 0)), whole(gain), whole(bias), whole(wt)],
        out_specs=pl.BlockSpec((64, 16, 128), lambda d: (0, 0, d)),
        scratch_shapes=[pltpu.VMEM((16 * 64, 128), F32)],
        compiler_params=pltpu.CompilerParams(vmem_limit_bytes=32 << 20),
        cost_estimate=pl.CostEstimate(flops=48 * 128 * 128 * 2 * 384, bytes_accessed=3 << 20, transcendentals=48 * 128 * 64),
    )(pieces, gain, bias, wt)


STEP = 8


def final_kernel(place_ref, *refs, subs, aliased):
    count = len(subs)
    lefts = [refs[4 * s : 4 * s + 3] for s in range(count)]
    gates = [refs[4 * s + 3] for s in range(count)]
    rest = refs[4 * count :]
    rights, rest = rest[:16], rest[16:]
    gain_ref, bias_ref, w_ref = rest[:3]
    out_ref, scratch = rest[3 + aliased :]
    rows = sum(subs)
    step = pl.program_id(0)
    block, core = place_ref[0], place_ref[1]
    for half in range(2):
        which = core if half == 0 else 1 - core
        for t in range(STEP):
            left = jnp.concatenate(
                [jnp.concatenate([ref[which, t] for ref in sub], axis=-1) for sub in lefts], axis=0
            )
            right = jnp.concatenate([rights[2 * n + half][t] for n in range(8)], axis=0)
            h = which * 64 + step * STEP + t
            scratch[pl.ds(pl.multiple_of(h * rows, rows), rows), :] = lax.dot_general(
                left, right, NT, preferred_element_type=F32
            )

    @pl.when(step == 64 // STEP - 1)
    def _():
        base = 0
        for sub, gate_ref in zip(subs, gates):

            def some_rows(q, _, base=base, gate_ref=gate_ref):
                parts = []
                for e in range(8):
                    x = scratch[pl.ds(base + q * 8 + e, 128, stride=rows), :]
                    centred = x - jnp.mean(x, axis=0, keepdims=True)
                    variance = jnp.mean(centred * centred, axis=0, keepdims=True)
                    parts.append(
                        (centred * lax.rsqrt(variance + EPSILON) * gain_ref[...] + bias_ref[...]).astype(BF16)
                    )
                y = jnp.concatenate(parts, axis=1)
                out = lax.dot_general(y, w_ref[...], TN, preferred_element_type=F32)
                for e in range(8):
                    for n in range(8):
                        chip = block ^ n
                        at = pl.ds(pl.multiple_of(chip % 4 * 32 + chip // 4 * 16, 16), 16)
                        mine = out[e * 128 + n * 16 : e * 128 + n * 16 + 16]
                        out_ref[base + q * 8 + e, at, :] = (gate_ref[q * 8 + e, at, :] * mine).astype(BF16)
                return 0

            lax.fori_loop(0, sub // 8, some_rows, 0)
            base += sub


def final(where, groups, rights, gain, bias, w_out, update, block):
    subs = tuple(g[3].shape[0] for g in groups)
    rows = sum(subs)
    operands, specs = [], []
    for l0, l1, l2, gate in groups:
        for l in (l0, l1, l2):
            operands.append(l.reshape(2, 64, gate.shape[0], 128))
            specs.append(pl.BlockSpec((2, STEP, gate.shape[0], 128), lambda s, _: (0, s, 0, 0)))
        operands.append(gate)
        specs.append(whole(gate))
    operands += rights
    specs += [pl.BlockSpec((STEP, 16, 384), lambda s, _: (s, 0, 0))] * 16
    operands += [gain, bias, w_out]
    specs += [whole(gain), whole(bias), whole(w_out)]
    aliases = {}
    if update is not None:
        aliases = {1 + len(operands): 0}
        operands.append(update)
        specs.append(pl.BlockSpec(memory_space=pl.ANY))
    return pl.pallas_call(
        functools.partial(final_kernel, subs=subs, aliased=len(aliases)),
        out_shape=jax.ShapeDtypeStruct((128, 128, 128), BF16),
        grid_spec=pltpu.PrefetchScalarGridSpec(
            num_scalar_prefetch=1,
            grid=(64 // STEP,),
            in_specs=specs,
            out_specs=pl.BlockSpec((rows, 128, 128), lambda s, _: (block, 0, 0)),
            scratch_shapes=[pltpu.VMEM((128 * rows, 128), F32)],
        ),
        input_output_aliases=aliases,
        compiler_params=pltpu.CompilerParams(vmem_limit_bytes=56 << 20),
        cost_estimate=pl.CostEstimate(
            flops=rows * 128 * 128 * 2 * 512, bytes_accessed=(14 << 20) + rows * 128 * 128 * 12, transcendentals=0
        ),
    )(where, *operands)


def shards(pair, ln_gain, ln_bias, w_proj, w_gate, out_gain, out_bias, w_out):
    row, col = lax.axis_index("row"), lax.axis_index("col")
    core, chip = row % 2, row // 2
    gain, bias = ln_gain[None, :], ln_bias[None, :]

    wt_left = w_proj[:, :256].T

    def left_of(part, source):
        return left_and_gate(source, *part, gain, bias, wt_left, w_gate)

    def one_back(value):
        return send(value, everyone(back))

    quarters = [pair[:32]] + [send(pair[32 * a : 32 * a + 32], scatter_pairs(a)) for a in (1, 2, 3)]
    big, big_gate = left_of(BIG, pair)
    big_once = one_back(big)
    quarters[1] = after(quarters[1], big)
    even = core == col % 2
    y, x_side = chip % 4, chip // 4

    def quarter_of(d):
        away = y ^ ((col - d) % 16 // 2 % 4)
        picked = quarters[0]
        for a in range(1, 4):
            picked = jnp.where(away == a, quarters[a], picked)
        return picked

    one = jnp.where(even, quarter_of(0), quarter_of(1))
    two = quarter_of(2)
    one_across = send(one[16:], across_pairs(False))
    two_across = send(two[16:], across_pairs(True))
    d_one = jnp.where(even, 0, 1)
    one = jnp.where(x_side == (col - d_one) % 16 // 8, one[:16], one_across)
    two = jnp.where(x_side == (col - 2) % 16 // 8, two[:16], two_across)
    moving = jnp.where(even, two, one)
    shifted = send(moving, shift_pairs())
    swapped_one = send(one, everyone(swap))
    small, small_gate = left_of(SMALL, after(pair, moving))
    small_once = one_back(small)
    shifted = after(shifted, big_once, swapped_one, small)
    big_twice = one_back(after(big_once, shifted))
    swapped = send(shifted, everyone(swap))
    first, swapped_first = one, swapped_one
    raw = jnp.concatenate(
        [
            jnp.where(even, first, swapped_first),
            jnp.where(even, swapped, shifted),
            jnp.where(even, shifted, swapped),
        ],
        axis=0,
    )
    half = [lax.dynamic_slice_in_dim(w_proj, 256 + 128 * v + 64 * core, 64, 1) for v in range(2)]
    mine = right_piece(raw, gain, bias, jnp.concatenate(half, axis=1).T)
    got = {0: mine}

    def exchange(value, n):
        return send(value, everyone(lambda r, c: (r ^ (2 * n), c)))

    for n in (4, 1, 3):
        got[n] = exchange(mine, n)
    stage = after(got[4], got[1], got[3], small_once)
    got[5], got[7] = exchange(stage, 1), exchange(stage, 3)
    got[2] = exchange(after(mine, stage), 2)
    small_twice = one_back(after(small_once, stage))
    stage = after(got[4], got[5], got[7], got[2])
    got[6] = exchange(stage, 2)
    rights = []
    for n in range(8):
        given = after(got[6], big_twice) if n == 6 else got[n]
        rights += [got[n], send(given, everyone(swap))]

    where = jnp.stack([chip ^ (col // 2), core]).astype(jnp.int32)
    out_g = jnp.broadcast_to(out_gain[:, None], (128, 128))
    out_b = jnp.broadcast_to(out_bias[:, None], (128, 128))

    groups = [(big, big_once, big_twice, big_gate), (small, small_once, small_twice, small_gate)]
    return final(where, groups, rights, out_g, out_b, w_out, None, 0)


def solution(mesh):
    in_specs = (P("row", "col", None), P(), P(), P(), P(), P(), P(), P())
    out_specs = P("row", "col", None)
    return jax.shard_map(shards, mesh=mesh, in_specs=in_specs, out_specs=out_specs, check_vma=False)
```

```python
import functools

import jax
import jax.numpy as jnp
from jax import lax
from jax.experimental import pallas as pl
from jax.experimental.pallas import tpu as pltpu
from jax.sharding import PartitionSpec as P

EPSILON = 1e-05
F32, BF16 = jnp.float32, jnp.bfloat16
NT = (((1,), (1,)), ((), ()))
TN = (((0,), (0,)), ((), ()))
AXES = ("row", "col")
BIG, SMALL = (0, 80), (80, 48)


def place(r, c):
    return (r % 16) * 16 + c % 16


def everyone(move):
    return [(place(r, c), place(*move(r, c))) for r in range(16) for c in range(16)]


def side(row):
    return row % 16 // 8


def scatter_pairs(a):
    return [(place(c, c + d), place(c ^ (2 * a), c + d)) for c in range(16) for d in range(3)]


def across_pairs(third):
    pairs = []
    for r in range(16):
        for c in range(16):
            even = (r - c) % 2 == 0
            d = 2 if third else 0 if even else 1
            if (even or not third) and side(r) == side(c - d):
                pairs.append((place(r, c), place(r ^ 8, c)))
    return pairs


def shift_pairs():
    return everyone(lambda r, c: (r, c - 2) if (r - c) % 2 == 0 else (r ^ 1, c - 1))


def back(r, c):
    return (r, c - 1)


def swap(r, c):
    return (r ^ 1, c)


def after(value, *others):
    return lax.optimization_barrier((value,) + others)[0]


def send(value, pairs):
    return lax.ppermute(value, AXES, pairs)


def sigmoid(x):
    return 0.5 * jnp.tanh(0.5 * x) + 0.5


def normed_rows(x, gain, bias):
    mean_of = jnp.full((128, 128), 1 / 128, BF16)
    centred = x.astype(F32) - jnp.dot(x, mean_of, preferred_element_type=F32)
    square = centred * centred
    high = square.astype(BF16)
    low = (square - high.astype(F32)).astype(BF16)
    variance = jnp.dot(high, mean_of, preferred_element_type=F32) + jnp.dot(
        low, mean_of, preferred_element_type=F32
    )
    return (centred * lax.rsqrt(variance + EPSILON) * gain + bias).astype(BF16)


def left_kernel(x_ref, gain_ref, bias_ref, wt_ref, wg_ref, left_ref, gate_ref, scratch):
    n = normed_rows(x_ref[...].reshape(16 * 128, 128), gain_ref[...], bias_ref[...])
    gate_ref[...] = sigmoid(jnp.dot(n, wg_ref[...], preferred_element_type=F32)).reshape(16, 128, 128)
    p = lax.dot_general(wt_ref[...], n, NT, preferred_element_type=F32)
    v = sigmoid(p[:128]) * p[128:]
    for i in range(16):
        scratch[i * 136 : i * 136 + 128, :] = v[:, i * 128 : (i + 1) * 128]

    def turn(h, _):
        left_ref[h] = scratch[pl.ds(h, 16, stride=136), :].astype(BF16)
        return 0

    lax.fori_loop(0, 128, turn, 0, unroll=16)


def whole(a):
    return pl.BlockSpec(a.shape, lambda *_: (0,) * a.ndim)


def left_and_gate(pair, start, rows, gain, bias, wt, w_gate):
    first = start // 16
    return pl.pallas_call(
        left_kernel,
        out_shape=[
            jax.ShapeDtypeStruct((128, rows, 128), BF16),
            jax.ShapeDtypeStruct((rows, 128, 128), F32),
        ],
        grid=(rows // 16,),
        in_specs=[
            pl.BlockSpec((16, 128, 128), lambda i: (first + i, 0, 0)),
            whole(gain),
            whole(bias),
            whole(wt),
            whole(w_gate),
        ],
        out_specs=[
            pl.BlockSpec((128, 16, 128), lambda i: (0, i, 0)),
            pl.BlockSpec((16, 128, 128), lambda i: (i, 0, 0)),
        ],
        scratch_shapes=[pltpu.VMEM((16 * 136, 128), F32)],
        compiler_params=pltpu.CompilerParams(vmem_limit_bytes=48 << 20),
        cost_estimate=pl.CostEstimate(
            flops=rows * 128 * 128 * 2 * 768, bytes_accessed=rows * 128 * 128 * 8, transcendentals=rows * 128 * 256
        ),
    )(pair, gain, bias, wt, w_gate)


def right_kernel(x_ref, gain_ref, bias_ref, wt_ref, right_ref, scratch):
    d = pl.program_id(0)
    n = normed_rows(x_ref[...].reshape(16 * 128, 128), gain_ref[...], bias_ref[...])
    p = lax.dot_general(wt_ref[...], n, NT, preferred_element_type=F32)
    v = sigmoid(p[:64]) * p[64:]
    for j in range(16):
        scratch[j * 72 : j * 72 + 64, :] = v[:, j * 128 : (j + 1) * 128]

    def turn(h, _):
        right_ref[h] = scratch[pl.ds(h, 16, stride=72), :].astype(BF16)
        return 0

    lax.fori_loop(0, 64, turn, 0, unroll=16)


def right_piece(pieces, gain, bias, wt):
    return pl.pallas_call(
        right_kernel,
        out_shape=jax.ShapeDtypeStruct((64, 16, 384), BF16),
        grid=(3,),
        in_specs=[pl.BlockSpec((16, 128, 128), lambda d: (d, 0, 0)), whole(gain), whole(bias), whole(wt)],
        out_specs=pl.BlockSpec((64, 16, 128), lambda d: (0, 0, d)),
        scratch_shapes=[pltpu.VMEM((16 * 72, 128), F32)],
        compiler_params=pltpu.CompilerParams(vmem_limit_bytes=32 << 20),
        cost_estimate=pl.CostEstimate(flops=48 * 128 * 128 * 2 * 384, bytes_accessed=3 << 20, transcendentals=48 * 128 * 64),
    )(pieces, gain, bias, wt)


STEP = 8


def final_kernel(place_ref, *refs, subs, aliased):
    count = len(subs)
    lefts = [refs[4 * s : 4 * s + 3] for s in range(count)]
    gates = [refs[4 * s + 3] for s in range(count)]
    rest = refs[4 * count :]
    rights, rest = rest[:16], rest[16:]
    gain_ref, bias_ref, w_ref = rest[:3]
    out_ref, scratch = rest[3 + aliased :]
    rows = sum(subs)
    step = pl.program_id(0)
    block, core = place_ref[0], place_ref[1]
    for half in range(2):
        which = core if half == 0 else 1 - core
        for t in range(STEP):
            left = jnp.concatenate(
                [jnp.concatenate([ref[which, t] for ref in sub], axis=-1) for sub in lefts], axis=0
            )
            right = jnp.concatenate([rights[2 * n + half][t] for n in range(8)], axis=0)
            h = which * 64 + step * STEP + t
            scratch[pl.ds(h * (rows + 1), rows), :] = lax.dot_general(
                left, right, NT, preferred_element_type=F32
            )

    @pl.when(step == 64 // STEP - 1)
    def _():
        base = 0
        for sub, gate_ref in zip(subs, gates):

            def some_rows(q, _, base=base, gate_ref=gate_ref):
                parts = []
                for e in range(16):
                    x = scratch[pl.ds(base + q * 16 + e, 128, stride=rows + 1), :]
                    centred = x - jnp.mean(x, axis=0, keepdims=True)
                    variance = jnp.mean(centred * centred, axis=0, keepdims=True)
                    parts.append(
                        (centred * lax.rsqrt(variance + EPSILON) * gain_ref[...] + bias_ref[...]).astype(BF16)
                    )
                y = jnp.concatenate(parts, axis=1)
                out = lax.dot_general(y, w_ref[...], TN, preferred_element_type=F32)
                for e in range(16):
                    for n in range(8):
                        chip = block ^ n
                        at = pl.ds(pl.multiple_of(chip % 4 * 32 + chip // 4 * 16, 16), 16)
                        mine = out[e * 128 + n * 16 : e * 128 + n * 16 + 16]
                        out_ref[base + q * 16 + e, at, :] = (gate_ref[q * 16 + e, at, :] * mine).astype(BF16)
                return 0

            lax.fori_loop(0, sub // 16, some_rows, 0)
            base += sub


def final(where, groups, rights, gain, bias, w_out, update, block):
    subs = tuple(g[3].shape[0] for g in groups)
    rows = sum(subs)
    operands, specs = [], []
    for l0, l1, l2, gate in groups:
        for l in (l0, l1, l2):
            operands.append(l.reshape(2, 64, gate.shape[0], 128))
            specs.append(pl.BlockSpec((2, STEP, gate.shape[0], 128), lambda s, _: (0, s, 0, 0)))
        operands.append(gate)
        specs.append(whole(gate))
    operands += rights
    specs += [pl.BlockSpec((STEP, 16, 384), lambda s, _: (s, 0, 0))] * 16
    operands += [gain, bias, w_out]
    specs += [whole(gain), whole(bias), whole(w_out)]
    aliases = {}
    if update is not None:
        aliases = {1 + len(operands): 0}
        operands.append(update)
        specs.append(pl.BlockSpec(memory_space=pl.ANY))
    return pl.pallas_call(
        functools.partial(final_kernel, subs=subs, aliased=len(aliases)),
        out_shape=jax.ShapeDtypeStruct((128, 128, 128), BF16),
        grid_spec=pltpu.PrefetchScalarGridSpec(
            num_scalar_prefetch=1,
            grid=(64 // STEP,),
            in_specs=specs,
            out_specs=pl.BlockSpec((rows, 128, 128), lambda s, _: (block, 0, 0)),
            scratch_shapes=[pltpu.VMEM((128 * (rows + 1), 128), F32)],
        ),
        input_output_aliases=aliases,
        compiler_params=pltpu.CompilerParams(vmem_limit_bytes=56 << 20),
        cost_estimate=pl.CostEstimate(
            flops=rows * 128 * 128 * 2 * 512, bytes_accessed=(14 << 20) + rows * 128 * 128 * 12, transcendentals=0
        ),
    )(where, *operands)


def shards(pair, ln_gain, ln_bias, w_proj, w_gate, out_gain, out_bias, w_out):
    row, col = lax.axis_index("row"), lax.axis_index("col")
    core, chip = row % 2, row // 2
    gain, bias = ln_gain[None, :], ln_bias[None, :]

    wt_left = w_proj[:, :256].T

    def left_of(part, source):
        return left_and_gate(source, *part, gain, bias, wt_left, w_gate)

    def one_back(value):
        return send(value, everyone(back))

    quarters = [pair[:32]] + [send(pair[32 * a : 32 * a + 32], scatter_pairs(a)) for a in (1, 2, 3)]
    big, big_gate = left_of(BIG, pair)
    big_once = one_back(big)
    small, small_gate = left_of(SMALL, pair)
    quarters[1] = after(quarters[1], big, small)
    even = core == col % 2
    y, x_side = chip % 4, chip // 4

    def quarter_of(d):
        away = y ^ ((col - d) % 16 // 2 % 4)
        picked = quarters[0]
        for a in range(1, 4):
            picked = jnp.where(away == a, quarters[a], picked)
        return picked

    one = jnp.where(even, quarter_of(0), quarter_of(1))
    two = quarter_of(2)
    one_across = send(one[16:], across_pairs(False))
    two_across = send(two[16:], across_pairs(True))
    d_one = jnp.where(even, 0, 1)
    one = jnp.where(x_side == (col - d_one) % 16 // 8, one[:16], one_across)
    two = jnp.where(x_side == (col - 2) % 16 // 8, two[:16], two_across)
    moving = jnp.where(even, two, one)
    shifted = send(moving, shift_pairs())
    swapped_one = send(one, everyone(swap))
    small_once = one_back(after(small, swapped_one))
    shifted = after(shifted, big_once, swapped_one, small)
    swapped = send(shifted, everyone(swap))
    first, swapped_first = one, swapped_one
    raw = jnp.concatenate(
        [
            jnp.where(even, first, swapped_first),
            jnp.where(even, swapped, shifted),
            jnp.where(even, shifted, swapped),
        ],
        axis=0,
    )
    half = [lax.dynamic_slice_in_dim(w_proj, 256 + 128 * v + 64 * core, 64, 1) for v in range(2)]
    mine = right_piece(raw, gain, bias, jnp.concatenate(half, axis=1).T)
    got = {0: mine}

    def exchange(value, n):
        return send(value, everyone(lambda r, c: (r ^ (2 * n), c)))

    swapped_mine = send(mine, everyone(swap))
    for n in (4, 1, 3):
        got[n] = exchange(mine, n)
    small_twice = one_back(after(small_once, swapped_mine))
    stage = after(got[4], got[1], got[3], small_once)
    got[5], got[7] = exchange(stage, 1), exchange(stage, 3)
    got[2] = exchange(after(mine, stage), 2)
    big_twice = one_back(after(big_once, stage))
    stage = after(got[4], got[5], got[7], got[2], small_twice)
    got[6] = exchange(stage, 2)
    rights = [mine, swapped_mine]
    for n in range(1, 8):
        rights += [got[n], send(got[n], everyone(swap))]

    where = jnp.stack([chip ^ (col // 2), core]).astype(jnp.int32)
    out_g = jnp.broadcast_to(out_gain[:, None], (128, 128))
    out_b = jnp.broadcast_to(out_bias[:, None], (128, 128))

    groups = [(big, big_once, big_twice, big_gate), (small, small_once, small_twice, small_gate)]
    return final(where, groups, rights, out_g, out_b, w_out, None, 0)


def solution(mesh):
    in_specs = (P("row", "col", None), P(), P(), P(), P(), P(), P(), P())
    out_specs = P("row", "col", None)
    return jax.shard_map(shards, mesh=mesh, in_specs=in_specs, out_specs=out_specs, check_vma=False)
```

```python
import functools

import jax
import jax.numpy as jnp
from jax import lax
from jax.experimental import pallas as pl
from jax.experimental.pallas import tpu as pltpu
from jax.sharding import PartitionSpec as P

EPSILON = 1e-05
F32, BF16 = jnp.float32, jnp.bfloat16
NT = (((1,), (1,)), ((), ()))
TN = (((0,), (0,)), ((), ()))
AXES = ("row", "col")
BIG, SMALL = (0, 96), (96, 32)


def place(r, c):
    return (r % 16) * 16 + c % 16


def everyone(move):
    return [(place(r, c), place(*move(r, c))) for r in range(16) for c in range(16)]


def side(row):
    return row % 16 // 8


def scatter_pairs(a):
    return [(place(c, c + d), place(c ^ (2 * a), c + d)) for c in range(16) for d in range(3)]


def across_pairs(third):
    pairs = []
    for r in range(16):
        for c in range(16):
            even = (r - c) % 2 == 0
            d = 2 if third else 0 if even else 1
            if (even or not third) and side(r) == side(c - d):
                pairs.append((place(r, c), place(r ^ 8, c)))
    return pairs


def shift_pairs():
    return everyone(lambda r, c: (r, c - 2) if (r - c) % 2 == 0 else (r ^ 1, c - 1))


def back(r, c):
    return (r, c - 1)


def swap(r, c):
    return (r ^ 1, c)


def after(value, *others):
    return lax.optimization_barrier((value,) + others)[0]


def send(value, pairs):
    return lax.ppermute(value, AXES, pairs)


def sigmoid(x):
    return 0.5 * jnp.tanh(0.5 * x) + 0.5


def normed_rows(x, gain, bias):
    mean_of = jnp.full((128, 128), 1 / 128, BF16)
    centred = x.astype(F32) - jnp.dot(x, mean_of, preferred_element_type=F32)
    square = centred * centred
    high = square.astype(BF16)
    low = (square - high.astype(F32)).astype(BF16)
    variance = jnp.dot(high, mean_of, preferred_element_type=F32) + jnp.dot(
        low, mean_of, preferred_element_type=F32
    )
    return (centred * lax.rsqrt(variance + EPSILON) * gain + bias).astype(BF16)


def left_kernel(x_ref, gain_ref, bias_ref, wt_ref, wg_ref, left_ref, gate_ref, scratch):
    n = normed_rows(x_ref[...].reshape(16 * 128, 128), gain_ref[...], bias_ref[...])
    gate_ref[...] = sigmoid(jnp.dot(n, wg_ref[...], preferred_element_type=F32)).reshape(16, 128, 128)
    p = lax.dot_general(wt_ref[...], n, NT, preferred_element_type=F32)
    v = sigmoid(p[:128]) * p[128:]
    for i in range(16):
        scratch[i * 136 : i * 136 + 128, :] = v[:, i * 128 : (i + 1) * 128]

    def turn(h, _):
        left_ref[h] = scratch[pl.ds(h, 16, stride=136), :].astype(BF16)
        return 0

    lax.fori_loop(0, 128, turn, 0, unroll=16)


def whole(a):
    return pl.BlockSpec(a.shape, lambda *_: (0,) * a.ndim)


def left_and_gate(pair, start, rows, gain, bias, wt, w_gate):
    first = start // 16
    return pl.pallas_call(
        left_kernel,
        out_shape=[
            jax.ShapeDtypeStruct((128, rows, 128), BF16),
            jax.ShapeDtypeStruct((rows, 128, 128), F32),
        ],
        grid=(rows // 16,),
        in_specs=[
            pl.BlockSpec((16, 128, 128), lambda i: (first + i, 0, 0)),
            whole(gain),
            whole(bias),
            whole(wt),
            whole(w_gate),
        ],
        out_specs=[
            pl.BlockSpec((128, 16, 128), lambda i: (0, i, 0)),
            pl.BlockSpec((16, 128, 128), lambda i: (i, 0, 0)),
        ],
        scratch_shapes=[pltpu.VMEM((16 * 136, 128), F32)],
        compiler_params=pltpu.CompilerParams(vmem_limit_bytes=48 << 20),
        cost_estimate=pl.CostEstimate(
            flops=rows * 128 * 128 * 2 * 768, bytes_accessed=rows * 128 * 128 * 8, transcendentals=rows * 128 * 256
        ),
    )(pair, gain, bias, wt, w_gate)


def right_kernel(x_ref, gain_ref, bias_ref, wt_ref, right_ref, scratch):
    d = pl.program_id(0)
    n = normed_rows(x_ref[...].reshape(16 * 128, 128), gain_ref[...], bias_ref[...])
    p = lax.dot_general(wt_ref[...], n, NT, preferred_element_type=F32)
    v = sigmoid(p[:64]) * p[64:]
    for j in range(16):
        scratch[j * 72 : j * 72 + 64, :] = v[:, j * 128 : (j + 1) * 128]

    def turn(h, _):
        right_ref[h] = scratch[pl.ds(h, 16, stride=72), :].astype(BF16)
        return 0

    lax.fori_loop(0, 64, turn, 0, unroll=16)


def right_piece(pieces, gain, bias, wt):
    return pl.pallas_call(
        right_kernel,
        out_shape=jax.ShapeDtypeStruct((64, 16, 384), BF16),
        grid=(3,),
        in_specs=[pl.BlockSpec((16, 128, 128), lambda d: (d, 0, 0)), whole(gain), whole(bias), whole(wt)],
        out_specs=pl.BlockSpec((64, 16, 128), lambda d: (0, 0, d)),
        scratch_shapes=[pltpu.VMEM((16 * 72, 128), F32)],
        compiler_params=pltpu.CompilerParams(vmem_limit_bytes=32 << 20),
        cost_estimate=pl.CostEstimate(flops=48 * 128 * 128 * 2 * 384, bytes_accessed=3 << 20, transcendentals=48 * 128 * 64),
    )(pieces, gain, bias, wt)


STEP = 8


def final_kernel(place_ref, *refs, subs, aliased):
    count = len(subs)
    lefts = [refs[4 * s : 4 * s + 3] for s in range(count)]
    gates = [refs[4 * s + 3] for s in range(count)]
    rest = refs[4 * count :]
    rights, rest = rest[:16], rest[16:]
    gain_ref, bias_ref, w_ref = rest[:3]
    out_ref, scratch = rest[3 + aliased :]
    rows = sum(subs)
    step = pl.program_id(0)
    block, core = place_ref[0], place_ref[1]
    for half in range(2):
        which = core if half == 0 else 1 - core
        for t in range(STEP):
            left = jnp.concatenate(
                [jnp.concatenate([ref[which, t] for ref in sub], axis=-1) for sub in lefts], axis=0
            )
            right = jnp.concatenate([rights[2 * n + half][t] for n in range(8)], axis=0)
            h = which * 64 + step * STEP + t
            scratch[pl.ds(h * (rows + 1), rows), :] = lax.dot_general(
                left, right, NT, preferred_element_type=F32
            )

    @pl.when(step == 64 // STEP - 1)
    def _():
        base = 0
        for sub, gate_ref in zip(subs, gates):

            def some_rows(q, _, base=base, gate_ref=gate_ref):
                parts = []
                for e in range(16):
                    x = scratch[pl.ds(base + q * 16 + e, 128, stride=rows + 1), :]
                    centred = x - jnp.mean(x, axis=0, keepdims=True)
                    variance = jnp.mean(centred * centred, axis=0, keepdims=True)
                    parts.append(
                        (centred * lax.rsqrt(variance + EPSILON) * gain_ref[...] + bias_ref[...]).astype(BF16)
                    )
                y = jnp.concatenate(parts, axis=1)
                out = lax.dot_general(y, w_ref[...], TN, preferred_element_type=F32)
                for e in range(16):
                    for n in range(8):
                        chip = block ^ n
                        at = pl.ds(pl.multiple_of(chip % 4 * 32 + chip // 4 * 16, 16), 16)
                        mine = out[e * 128 + n * 16 : e * 128 + n * 16 + 16]
                        out_ref[base + q * 16 + e, at, :] = (gate_ref[q * 16 + e, at, :] * mine).astype(BF16)
                return 0

            lax.fori_loop(0, sub // 16, some_rows, 0)
            base += sub


def final(where, groups, rights, gain, bias, w_out, update, block):
    subs = tuple(g[3].shape[0] for g in groups)
    rows = sum(subs)
    operands, specs = [], []
    for l0, l1, l2, gate in groups:
        for l in (l0, l1, l2):
            operands.append(l.reshape(2, 64, gate.shape[0], 128))
            specs.append(pl.BlockSpec((2, STEP, gate.shape[0], 128), lambda s, _: (0, s, 0, 0)))
        operands.append(gate)
        specs.append(whole(gate))
    operands += rights
    specs += [pl.BlockSpec((STEP, 16, 384), lambda s, _: (s, 0, 0))] * 16
    operands += [gain, bias, w_out]
    specs += [whole(gain), whole(bias), whole(w_out)]
    aliases = {}
    if update is not None:
        aliases = {1 + len(operands): 0}
        operands.append(update)
        specs.append(pl.BlockSpec(memory_space=pl.ANY))
    return pl.pallas_call(
        functools.partial(final_kernel, subs=subs, aliased=len(aliases)),
        out_shape=jax.ShapeDtypeStruct((128, 128, 128), BF16),
        grid_spec=pltpu.PrefetchScalarGridSpec(
            num_scalar_prefetch=1,
            grid=(64 // STEP,),
            in_specs=specs,
            out_specs=pl.BlockSpec((rows, 128, 128), lambda s, _: (block, 0, 0)),
            scratch_shapes=[pltpu.VMEM((128 * (rows + 1), 128), F32)],
        ),
        input_output_aliases=aliases,
        compiler_params=pltpu.CompilerParams(vmem_limit_bytes=56 << 20),
        cost_estimate=pl.CostEstimate(
            flops=rows * 128 * 128 * 2 * 512, bytes_accessed=(14 << 20) + rows * 128 * 128 * 12, transcendentals=0
        ),
    )(where, *operands)


def shards(pair, ln_gain, ln_bias, w_proj, w_gate, out_gain, out_bias, w_out):
    row, col = lax.axis_index("row"), lax.axis_index("col")
    core, chip = row % 2, row // 2
    gain, bias = ln_gain[None, :], ln_bias[None, :]

    wt_left = w_proj[:, :256].T

    def left_of(part, source):
        return left_and_gate(source, *part, gain, bias, wt_left, w_gate)

    def one_back(value):
        return send(value, everyone(back))

    quarters = [pair[:32]] + [send(pair[32 * a : 32 * a + 32], scatter_pairs(a)) for a in (1, 2, 3)]
    big, big_gate = left_of(BIG, pair)
    big_once = one_back(big)
    small, small_gate = left_of(SMALL, pair)
    quarters[1] = after(quarters[1], big, small)
    even = core == col % 2
    y, x_side = chip % 4, chip // 4

    def quarter_of(d):
        away = y ^ ((col - d) % 16 // 2 % 4)
        picked = quarters[0]
        for a in range(1, 4):
            picked = jnp.where(away == a, quarters[a], picked)
        return picked

    one = jnp.where(even, quarter_of(0), quarter_of(1))
    two = quarter_of(2)
    one_across = send(one[16:], across_pairs(False))
    two_across = send(two[16:], across_pairs(True))
    d_one = jnp.where(even, 0, 1)
    one = jnp.where(x_side == (col - d_one) % 16 // 8, one[:16], one_across)
    two = jnp.where(x_side == (col - 2) % 16 // 8, two[:16], two_across)
    moving = jnp.where(even, two, one)
    shifted = send(moving, shift_pairs())
    swapped_one = send(one, everyone(swap))
    small_once = one_back(after(small, swapped_one))
    shifted = after(shifted, big_once, swapped_one, small)
    swapped = send(shifted, everyone(swap))
    first, swapped_first = one, swapped_one
    raw = jnp.concatenate(
        [
            jnp.where(even, first, swapped_first),
            jnp.where(even, swapped, shifted),
            jnp.where(even, shifted, swapped),
        ],
        axis=0,
    )
    half = [lax.dynamic_slice_in_dim(w_proj, 256 + 128 * v + 64 * core, 64, 1) for v in range(2)]
    mine = right_piece(raw, gain, bias, jnp.concatenate(half, axis=1).T)
    got = {0: mine}

    def exchange(value, n):
        return send(value, everyone(lambda r, c: (r ^ (2 * n), c)))

    swapped_mine = send(mine, everyone(swap))
    for n in (4, 1, 3):
        got[n] = exchange(mine, n)
    stage = after(got[4], got[1], got[3], small_once)
    got[5], got[7] = exchange(stage, 1), exchange(stage, 3)
    got[2] = exchange(after(mine, stage), 2)
    big_twice = one_back(after(big_once, stage))
    small_twice = one_back(after(small_once, got[5], got[2]))
    stage = after(got[4], got[5], got[7], got[2])
    got[6] = exchange(stage, 2)
    rights = [mine, swapped_mine]
    for n in range(1, 8):
        rights += [got[n], send(got[n], everyone(swap))]

    where = jnp.stack([chip ^ (col // 2), core]).astype(jnp.int32)
    out_g = jnp.broadcast_to(out_gain[:, None], (128, 128))
    out_b = jnp.broadcast_to(out_bias[:, None], (128, 128))

    groups = [(big, big_once, big_twice, big_gate), (small, small_once, small_twice, small_gate)]
    return final(where, groups, rights, out_g, out_b, w_out, None, 0)


def solution(mesh):
    in_specs = (P("row", "col", None), P(), P(), P(), P(), P(), P(), P())
    out_specs = P("row", "col", None)
    return jax.shard_map(shards, mesh=mesh, in_specs=in_specs, out_specs=out_specs, check_vma=False)
```

```python
import functools

import jax
import jax.numpy as jnp
from jax import lax
from jax.experimental import pallas as pl
from jax.experimental.pallas import tpu as pltpu
from jax.sharding import PartitionSpec as P

EPSILON = 1e-05
F32, BF16 = jnp.float32, jnp.bfloat16
NT = (((1,), (1,)), ((), ()))
TN = (((0,), (0,)), ((), ()))
AXES = ("row", "col")
BIG, SMALL, RING = (0, 96), (96, 16), (112, 16)


def place(r, c):
    return (r % 16) * 16 + c % 16


def everyone(move):
    return [(place(r, c), place(*move(r, c))) for r in range(16) for c in range(16)]


def after_hops(c, hops):
    return (c - 8 + hops) % 16 if hops >= 6 else c // 8 * 8 + (c + hops) % 8


def ring_pairs(hop):
    return everyone_from(lambda c: after_hops(c, hop - 1), lambda c: after_hops(c, hop))


def everyone_from(source, target):
    return [(place(r, source(c)), place(r, target(c))) for r in range(16) for c in range(16)]


def side(row):
    return row % 16 // 8


def scatter_pairs(a):
    return [(place(c, c + d), place(c ^ (2 * a), c + d)) for c in range(16) for d in range(3)]


def across_pairs(third):
    pairs = []
    for r in range(16):
        for c in range(16):
            even = (r - c) % 2 == 0
            d = 2 if third else 0 if even else 1
            if (even or not third) and side(r) == side(c - d):
                pairs.append((place(r, c), place(r ^ 8, c)))
    return pairs


def shift_pairs():
    return everyone(lambda r, c: (r, c - 2) if (r - c) % 2 == 0 else (r ^ 1, c - 1))


def back(r, c):
    return (r, c - 1)


def swap(r, c):
    return (r ^ 1, c)


def after(value, *others):
    return lax.optimization_barrier((value,) + others)[0]


def send(value, pairs):
    return lax.ppermute(value, AXES, pairs)


def sigmoid(x):
    return 0.5 * jnp.tanh(0.5 * x) + 0.5


def normed_rows(x, gain, bias):
    mean_of = jnp.full((128, 128), 1 / 128, BF16)
    centred = x.astype(F32) - jnp.dot(x, mean_of, preferred_element_type=F32)
    square = centred * centred
    high = square.astype(BF16)
    low = (square - high.astype(F32)).astype(BF16)
    variance = jnp.dot(high, mean_of, preferred_element_type=F32) + jnp.dot(
        low, mean_of, preferred_element_type=F32
    )
    return (centred * lax.rsqrt(variance + EPSILON) * gain + bias).astype(BF16)


def left_kernel(x_ref, gain_ref, bias_ref, wt_ref, wg_ref, left_ref, gate_ref, scratch):
    n = normed_rows(x_ref[...].reshape(16 * 128, 128), gain_ref[...], bias_ref[...])
    gate_ref[...] = sigmoid(jnp.dot(n, wg_ref[...], preferred_element_type=F32)).reshape(16, 128, 128)
    p = lax.dot_general(wt_ref[...], n, NT, preferred_element_type=F32)
    v = sigmoid(p[:128]) * p[128:]
    for i in range(16):
        scratch[i * 136 : i * 136 + 128, :] = v[:, i * 128 : (i + 1) * 128]

    def turn(h, _):
        left_ref[h] = scratch[pl.ds(h, 16, stride=136), :].astype(BF16)
        return 0

    lax.fori_loop(0, 128, turn, 0, unroll=16)


def whole(a):
    return pl.BlockSpec(a.shape, lambda *_: (0,) * a.ndim)


def left_and_gate(pair, start, rows, gain, bias, wt, w_gate):
    first = start // 16
    return pl.pallas_call(
        left_kernel,
        out_shape=[
            jax.ShapeDtypeStruct((128, rows, 128), BF16),
            jax.ShapeDtypeStruct((rows, 128, 128), F32),
        ],
        grid=(rows // 16,),
        in_specs=[
            pl.BlockSpec((16, 128, 128), lambda i: (first + i, 0, 0)),
            whole(gain),
            whole(bias),
            whole(wt),
            whole(w_gate),
        ],
        out_specs=[
            pl.BlockSpec((128, 16, 128), lambda i: (0, i, 0)),
            pl.BlockSpec((16, 128, 128), lambda i: (i, 0, 0)),
        ],
        scratch_shapes=[pltpu.VMEM((16 * 136, 128), F32)],
        compiler_params=pltpu.CompilerParams(vmem_limit_bytes=48 << 20),
        cost_estimate=pl.CostEstimate(
            flops=rows * 128 * 128 * 2 * 768, bytes_accessed=rows * 128 * 128 * 8, transcendentals=rows * 128 * 256
        ),
    )(pair, gain, bias, wt, w_gate)


def right_kernel(x_ref, gain_ref, bias_ref, wt_ref, right_ref, scratch):
    d = pl.program_id(0)
    n = normed_rows(x_ref[...].reshape(16 * 128, 128), gain_ref[...], bias_ref[...])
    p = lax.dot_general(wt_ref[...], n, NT, preferred_element_type=F32)
    v = sigmoid(p[:64]) * p[64:]
    for j in range(16):
        scratch[j * 72 : j * 72 + 64, :] = v[:, j * 128 : (j + 1) * 128]

    def turn(h, _):
        right_ref[h] = scratch[pl.ds(h, 16, stride=72), :].astype(BF16)
        return 0

    lax.fori_loop(0, 64, turn, 0, unroll=16)


def right_piece(pieces, gain, bias, wt):
    return pl.pallas_call(
        right_kernel,
        out_shape=jax.ShapeDtypeStruct((64, 16, 384), BF16),
        grid=(3,),
        in_specs=[pl.BlockSpec((16, 128, 128), lambda d: (d, 0, 0)), whole(gain), whole(bias), whole(wt)],
        out_specs=pl.BlockSpec((64, 16, 128), lambda d: (0, 0, d)),
        scratch_shapes=[pltpu.VMEM((16 * 72, 128), F32)],
        compiler_params=pltpu.CompilerParams(vmem_limit_bytes=32 << 20),
        cost_estimate=pl.CostEstimate(flops=48 * 128 * 128 * 2 * 384, bytes_accessed=3 << 20, transcendentals=48 * 128 * 64),
    )(pieces, gain, bias, wt)


STEP = 8


def final_kernel(place_ref, *refs, subs, aliased):
    count = len(subs)
    lefts = [refs[4 * s : 4 * s + 3] for s in range(count)]
    gates = [refs[4 * s + 3] for s in range(count)]
    rest = refs[4 * count :]
    rights, rest = rest[:16], rest[16:]
    gain_ref, bias_ref, w_ref = rest[:3]
    out_ref, scratch = rest[3 + aliased :]
    rows = sum(subs)
    step = pl.program_id(0)
    block, core = place_ref[0], place_ref[1]
    for half in range(2):
        which = core if half == 0 else 1 - core
        for t in range(STEP):
            left = jnp.concatenate(
                [jnp.concatenate([ref[which, t] for ref in sub], axis=-1) for sub in lefts], axis=0
            )
            right = jnp.concatenate([rights[2 * n + half][t] for n in range(8)], axis=0)
            h = which * 64 + step * STEP + t
            scratch[pl.ds(h * (rows + 1), rows), :] = lax.dot_general(
                left, right, NT, preferred_element_type=F32
            )

    @pl.when(step == 64 // STEP - 1)
    def _():
        base = 0
        for sub, gate_ref in zip(subs, gates):

            def some_rows(q, _, base=base, gate_ref=gate_ref):
                parts = []
                for e in range(16):
                    x = scratch[pl.ds(base + q * 16 + e, 128, stride=rows + 1), :]
                    centred = x - jnp.mean(x, axis=0, keepdims=True)
                    variance = jnp.mean(centred * centred, axis=0, keepdims=True)
                    parts.append(
                        (centred * lax.rsqrt(variance + EPSILON) * gain_ref[...] + bias_ref[...]).astype(BF16)
                    )
                y = jnp.concatenate(parts, axis=1)
                out = lax.dot_general(y, w_ref[...], TN, preferred_element_type=F32)
                for e in range(16):
                    for n in range(8):
                        chip = block ^ n
                        at = pl.ds(pl.multiple_of(chip % 4 * 32 + chip // 4 * 16, 16), 16)
                        mine = out[e * 128 + n * 16 : e * 128 + n * 16 + 16]
                        out_ref[base + q * 16 + e, at, :] = (gate_ref[q * 16 + e, at, :] * mine).astype(BF16)
                return 0

            lax.fori_loop(0, sub // 16, some_rows, 0)
            base += sub


def final(where, groups, rights, gain, bias, w_out, update, block):
    subs = tuple(g[3].shape[0] for g in groups)
    rows = sum(subs)
    operands, specs = [], []
    for l0, l1, l2, gate in groups:
        for l in (l0, l1, l2):
            operands.append(l.reshape(2, 64, gate.shape[0], 128))
            specs.append(pl.BlockSpec((2, STEP, gate.shape[0], 128), lambda s, _: (0, s, 0, 0)))
        operands.append(gate)
        specs.append(whole(gate))
    operands += rights
    specs += [pl.BlockSpec((STEP, 16, 384), lambda s, _: (s, 0, 0))] * 16
    operands += [gain, bias, w_out]
    specs += [whole(gain), whole(bias), whole(w_out)]
    aliases = {}
    if update is not None:
        aliases = {1 + len(operands): 0}
        operands.append(update)
        specs.append(pl.BlockSpec(memory_space=pl.ANY))
    return pl.pallas_call(
        functools.partial(final_kernel, subs=subs, aliased=len(aliases)),
        out_shape=jax.ShapeDtypeStruct((128, 128, 128), BF16),
        grid_spec=pltpu.PrefetchScalarGridSpec(
            num_scalar_prefetch=1,
            grid=(64 // STEP,),
            in_specs=specs,
            out_specs=pl.BlockSpec((rows, 128, 128), lambda s, _: (block, 0, 0)),
            scratch_shapes=[pltpu.VMEM((128 * (rows + 1), 128), F32)],
        ),
        input_output_aliases=aliases,
        compiler_params=pltpu.CompilerParams(vmem_limit_bytes=56 << 20),
        cost_estimate=pl.CostEstimate(
            flops=rows * 128 * 128 * 2 * 512, bytes_accessed=(14 << 20) + rows * 128 * 128 * 12, transcendentals=0
        ),
    )(where, *operands)


def shards(pair, ln_gain, ln_bias, w_proj, w_gate, out_gain, out_bias, w_out):
    row, col = lax.axis_index("row"), lax.axis_index("col")
    core, chip = row % 2, row // 2
    gain, bias = ln_gain[None, :], ln_bias[None, :]

    wt_left = w_proj[:, :256].T

    def left_of(part, source):
        return left_and_gate(source, *part, gain, bias, wt_left, w_gate)

    def one_back(value):
        return send(value, everyone(back))

    quarters = [pair[:32]] + [send(pair[32 * a : 32 * a + 32], scatter_pairs(a)) for a in (1, 2, 3)]
    big, big_gate = left_of(BIG, pair)
    big_once = one_back(big)
    small, small_gate = left_of(SMALL, pair)
    whirl, whirl_gate = left_of(RING, pair)
    ring = [whirl, send(whirl, ring_pairs(1))]
    quarters[1] = after(quarters[1], big, small, whirl)
    even = core == col % 2
    y, x_side = chip % 4, chip // 4

    def quarter_of(d):
        away = y ^ ((col - d) % 16 // 2 % 4)
        picked = quarters[0]
        for a in range(1, 4):
            picked = jnp.where(away == a, quarters[a], picked)
        return picked

    one = jnp.where(even, quarter_of(0), quarter_of(1))
    two = quarter_of(2)
    ring.append(send(after(ring[1], two), ring_pairs(2)))
    one_across = send(one[16:], across_pairs(False))
    two_across = send(two[16:], across_pairs(True))
    d_one = jnp.where(even, 0, 1)
    one = jnp.where(x_side == (col - d_one) % 16 // 8, one[:16], one_across)
    two = jnp.where(x_side == (col - 2) % 16 // 8, two[:16], two_across)
    moving = after(jnp.where(even, two, one), ring[1])
    ring.append(send(after(ring[2], moving), ring_pairs(3)))
    shifted = send(moving, shift_pairs())
    swapped_one = send(one, everyone(swap))
    small_once = one_back(after(small, swapped_one))
    shifted = after(shifted, big_once, swapped_one, small, ring[2])
    ring.append(send(after(ring[3], shifted), ring_pairs(4)))
    swapped = send(shifted, everyone(swap))
    first, swapped_first = one, swapped_one
    raw = jnp.concatenate(
        [
            jnp.where(even, first, swapped_first),
            jnp.where(even, swapped, shifted),
            jnp.where(even, shifted, swapped),
        ],
        axis=0,
    )
    half = [lax.dynamic_slice_in_dim(w_proj, 256 + 128 * v + 64 * core, 64, 1) for v in range(2)]
    mine = right_piece(raw, gain, bias, jnp.concatenate(half, axis=1).T)
    mine = after(mine, ring[3])
    ring.append(send(after(ring[4], mine), ring_pairs(5)))
    got = {0: mine}

    def exchange(value, n):
        return send(value, everyone(lambda r, c: (r ^ (2 * n), c)))

    swapped_mine = send(mine, everyone(swap))
    for n in (4, 1, 3):
        got[n] = exchange(mine, n)
    stage = after(got[4], got[1], got[3], small_once, ring[4])
    got[5], got[7] = exchange(stage, 1), exchange(stage, 3)
    got[2] = exchange(after(mine, stage), 2)
    big_twice = one_back(after(big_once, stage))
    small_twice = one_back(after(small_once, got[5], got[2]))
    stage = after(got[4], got[5], got[7], got[2], ring[5])
    ring.append(send(after(ring[5], stage), ring_pairs(6)))
    got[6] = exchange(stage, 2)
    ring.append(send(after(ring[6], got[6]), ring_pairs(7)))
    rights = [mine, swapped_mine]
    for n in range(1, 8):
        rights += [got[n], send(got[n], everyone(swap))]

    where = jnp.stack([chip ^ (col // 2), core]).astype(jnp.int32)
    out_g = jnp.broadcast_to(out_gain[:, None], (128, 128))
    out_b = jnp.broadcast_to(out_bias[:, None], (128, 128))

    groups = [(big, big_once, big_twice, big_gate), (small, small_once, small_twice, small_gate)]
    groups.append((whirl, ring[7], ring[6], whirl_gate))
    return final(where, groups, rights, out_g, out_b, w_out, None, 0)


def solution(mesh):
    in_specs = (P("row", "col", None), P(), P(), P(), P(), P(), P(), P())
    out_specs = P("row", "col", None)
    return jax.shard_map(shards, mesh=mesh, in_specs=in_specs, out_specs=out_specs, check_vma=False)
```

```python
import functools

import jax
import jax.numpy as jnp
from jax import lax
from jax.experimental import pallas as pl
from jax.experimental.pallas import tpu as pltpu
from jax.sharding import PartitionSpec as P

EPSILON = 1e-05
F32, BF16 = jnp.float32, jnp.bfloat16
NT = (((1,), (1,)), ((), ()))
TN = (((0,), (0,)), ((), ()))
AXES = ("row", "col")
BIG, SMALL, RING = (0, 96), (96, 16), (112, 16)


def place(r, c):
    return (r % 16) * 16 + c % 16


def everyone(move):
    return [(place(r, c), place(*move(r, c))) for r in range(16) for c in range(16)]


def after_hops(c, hops):
    return (c - 8 + hops) % 16 if hops >= 6 else c // 8 * 8 + (c + hops) % 8


def ring_pairs(hop):
    return everyone_from(lambda c: after_hops(c, hop - 1), lambda c: after_hops(c, hop))


def everyone_from(source, target):
    return [(place(r, source(c)), place(r, target(c))) for r in range(16) for c in range(16)]


def side(row):
    return row % 16 // 8


def scatter_pairs(a):
    return [(place(c, c + d), place(c ^ (2 * a), c + d)) for c in range(16) for d in range(3)]


def across_pairs(third):
    pairs = []
    for r in range(16):
        for c in range(16):
            even = (r - c) % 2 == 0
            d = 2 if third else 0 if even else 1
            if (even or not third) and side(r) == side(c - d):
                pairs.append((place(r, c), place(r ^ 8, c)))
    return pairs


def shift_pairs():
    return everyone(lambda r, c: (r, c - 2) if (r - c) % 2 == 0 else (r ^ 1, c - 1))


def back(r, c):
    return (r, c - 1)


def swap(r, c):
    return (r ^ 1, c)


def after(value, *others):
    return lax.optimization_barrier((value,) + others)[0]


def send(value, pairs):
    return lax.ppermute(value, AXES, pairs)


def sigmoid(x):
    return 0.5 * jnp.tanh(0.5 * x) + 0.5


def normed_rows(x, gain, bias):
    mean_of = jnp.full((128, 128), 1 / 128, BF16)
    centred = x.astype(F32) - jnp.dot(x, mean_of, preferred_element_type=F32)
    square = centred * centred
    high = square.astype(BF16)
    low = (square - high.astype(F32)).astype(BF16)
    variance = jnp.dot(high, mean_of, preferred_element_type=F32) + jnp.dot(
        low, mean_of, preferred_element_type=F32
    )
    return (centred * lax.rsqrt(variance + EPSILON) * gain + bias).astype(BF16)


def left_kernel(x_ref, gain_ref, bias_ref, wt_ref, wg_ref, left_ref, gate_ref, scratch):
    n = normed_rows(x_ref[...].reshape(16 * 128, 128), gain_ref[...], bias_ref[...])
    gate_ref[...] = sigmoid(jnp.dot(n, wg_ref[...], preferred_element_type=F32)).reshape(16, 128, 128)
    p = lax.dot_general(wt_ref[...], n, NT, preferred_element_type=F32)
    v = sigmoid(p[:128]) * p[128:]
    for i in range(16):
        scratch[i * 136 : i * 136 + 128, :] = v[:, i * 128 : (i + 1) * 128]

    def turn(h, _):
        left_ref[h] = scratch[pl.ds(h, 16, stride=136), :].astype(BF16)
        return 0

    lax.fori_loop(0, 128, turn, 0, unroll=16)


def whole(a):
    return pl.BlockSpec(a.shape, lambda *_: (0,) * a.ndim)


def left_and_gate(pair, start, rows, gain, bias, wt, w_gate):
    first = start // 16
    return pl.pallas_call(
        left_kernel,
        out_shape=[
            jax.ShapeDtypeStruct((128, rows, 128), BF16),
            jax.ShapeDtypeStruct((rows, 128, 128), F32),
        ],
        grid=(rows // 16,),
        in_specs=[
            pl.BlockSpec((16, 128, 128), lambda i: (first + i, 0, 0)),
            whole(gain),
            whole(bias),
            whole(wt),
            whole(w_gate),
        ],
        out_specs=[
            pl.BlockSpec((128, 16, 128), lambda i: (0, i, 0)),
            pl.BlockSpec((16, 128, 128), lambda i: (i, 0, 0)),
        ],
        scratch_shapes=[pltpu.VMEM((16 * 136, 128), F32)],
        compiler_params=pltpu.CompilerParams(vmem_limit_bytes=48 << 20),
        cost_estimate=pl.CostEstimate(
            flops=rows * 128 * 128 * 2 * 768, bytes_accessed=rows * 128 * 128 * 8, transcendentals=rows * 128 * 256
        ),
    )(pair, gain, bias, wt, w_gate)


def right_kernel(x_ref, gain_ref, bias_ref, wt_ref, right_ref, scratch):
    d = pl.program_id(0)
    n = normed_rows(x_ref[...].reshape(16 * 128, 128), gain_ref[...], bias_ref[...])
    p = lax.dot_general(wt_ref[...], n, NT, preferred_element_type=F32)
    v = sigmoid(p[:64]) * p[64:]
    for j in range(16):
        scratch[j * 72 : j * 72 + 64, :] = v[:, j * 128 : (j + 1) * 128]

    def turn(h, _):
        right_ref[h] = scratch[pl.ds(h, 16, stride=72), :].astype(BF16)
        return 0

    lax.fori_loop(0, 64, turn, 0, unroll=16)


def right_piece(pieces, gain, bias, wt):
    return pl.pallas_call(
        right_kernel,
        out_shape=jax.ShapeDtypeStruct((64, 16, 384), BF16),
        grid=(3,),
        in_specs=[pl.BlockSpec((16, 128, 128), lambda d: (d, 0, 0)), whole(gain), whole(bias), whole(wt)],
        out_specs=pl.BlockSpec((64, 16, 128), lambda d: (0, 0, d)),
        scratch_shapes=[pltpu.VMEM((16 * 72, 128), F32)],
        compiler_params=pltpu.CompilerParams(vmem_limit_bytes=32 << 20),
        cost_estimate=pl.CostEstimate(flops=48 * 128 * 128 * 2 * 384, bytes_accessed=3 << 20, transcendentals=48 * 128 * 64),
    )(pieces, gain, bias, wt)


STEP = 8


def final_kernel(place_ref, *refs, subs, aliased):
    count = len(subs)
    lefts = [refs[4 * s : 4 * s + 3] for s in range(count)]
    gates = [refs[4 * s + 3] for s in range(count)]
    rest = refs[4 * count :]
    rights, rest = rest[:16], rest[16:]
    gain_ref, bias_ref, w_ref = rest[:3]
    out_ref, scratch = rest[3 + aliased :]
    rows = sum(subs)
    step = pl.program_id(0)
    block, core = place_ref[0], place_ref[1]
    for half in range(2):
        which = core if half == 0 else 1 - core
        for t in range(STEP):
            left = jnp.concatenate(
                [jnp.concatenate([ref[which, t] for ref in sub], axis=-1) for sub in lefts], axis=0
            )
            right = jnp.concatenate([rights[2 * n + half][t] for n in range(8)], axis=0)
            h = which * 64 + step * STEP + t
            scratch[pl.ds(h * (rows + 1), rows), :] = lax.dot_general(
                left, right, NT, preferred_element_type=F32
            )

    @pl.when(step == 64 // STEP - 1)
    def _():
        base = 0
        for sub, gate_ref in zip(subs, gates):

            def some_rows(q, _, base=base, gate_ref=gate_ref):
                parts = []
                for e in range(16):
                    x = scratch[pl.ds(base + q * 16 + e, 128, stride=rows + 1), :]
                    centred = x - jnp.mean(x, axis=0, keepdims=True)
                    variance = jnp.mean(centred * centred, axis=0, keepdims=True)
                    parts.append(
                        (centred * lax.rsqrt(variance + EPSILON) * gain_ref[...] + bias_ref[...]).astype(BF16)
                    )
                y = jnp.concatenate(parts, axis=1)
                out = lax.dot_general(y, w_ref[...], TN, preferred_element_type=F32)
                for e in range(16):
                    for n in range(8):
                        chip = block ^ n
                        at = pl.ds(pl.multiple_of(chip % 4 * 32 + chip // 4 * 16, 16), 16)
                        mine = out[e * 128 + n * 16 : e * 128 + n * 16 + 16]
                        out_ref[base + q * 16 + e, at, :] = (gate_ref[q * 16 + e, at, :] * mine).astype(BF16)
                return 0

            lax.fori_loop(0, sub // 16, some_rows, 0)
            base += sub


def final(where, groups, rights, gain, bias, w_out, update, block):
    subs = tuple(g[3].shape[0] for g in groups)
    rows = sum(subs)
    operands, specs = [], []
    for l0, l1, l2, gate in groups:
        for l in (l0, l1, l2):
            operands.append(l.reshape(2, 64, gate.shape[0], 128))
            specs.append(pl.BlockSpec((2, STEP, gate.shape[0], 128), lambda s, _: (0, s, 0, 0)))
        operands.append(gate)
        specs.append(whole(gate))
    operands += rights
    specs += [pl.BlockSpec((STEP, 16, 384), lambda s, _: (s, 0, 0))] * 16
    operands += [gain, bias, w_out]
    specs += [whole(gain), whole(bias), whole(w_out)]
    aliases = {}
    if update is not None:
        aliases = {1 + len(operands): 0}
        operands.append(update)
        specs.append(pl.BlockSpec(memory_space=pl.ANY))
    return pl.pallas_call(
        functools.partial(final_kernel, subs=subs, aliased=len(aliases)),
        out_shape=jax.ShapeDtypeStruct((128, 128, 128), BF16),
        grid_spec=pltpu.PrefetchScalarGridSpec(
            num_scalar_prefetch=1,
            grid=(64 // STEP,),
            in_specs=specs,
            out_specs=pl.BlockSpec((rows, 128, 128), lambda s, _: (block, 0, 0)),
            scratch_shapes=[pltpu.VMEM((128 * (rows + 1), 128), F32)],
        ),
        input_output_aliases=aliases,
        compiler_params=pltpu.CompilerParams(vmem_limit_bytes=56 << 20),
        cost_estimate=pl.CostEstimate(
            flops=rows * 128 * 128 * 2 * 512, bytes_accessed=(14 << 20) + rows * 128 * 128 * 12, transcendentals=0
        ),
    )(where, *operands)


def shards(pair, ln_gain, ln_bias, w_proj, w_gate, out_gain, out_bias, w_out):
    row, col = lax.axis_index("row"), lax.axis_index("col")
    core, chip = row % 2, row // 2
    gain, bias = ln_gain[None, :], ln_bias[None, :]

    wt_left = w_proj[:, :256].T

    def left_of(part, source):
        return left_and_gate(source, *part, gain, bias, wt_left, w_gate)

    def one_back(value):
        return send(value, everyone(back))

    quarters = [pair[:32]] + [send(pair[32 * a : 32 * a + 32], scatter_pairs(a)) for a in (1, 2, 3)]
    big, big_gate = left_of(BIG, pair)
    big_once = one_back(big)
    small, small_gate = left_of(SMALL, pair)
    whirl, whirl_gate = left_of(RING, pair)
    ring = [whirl, send(whirl, ring_pairs(1))]
    quarters[1] = after(quarters[1], big, small, whirl)
    even = core == col % 2
    y, x_side = chip % 4, chip // 4

    def quarter_of(d):
        away = y ^ ((col - d) % 16 // 2 % 4)
        picked = quarters[0]
        for a in range(1, 4):
            picked = jnp.where(away == a, quarters[a], picked)
        return picked

    one = jnp.where(even, quarter_of(0), quarter_of(1))
    two = quarter_of(2)
    ring.append(send(after(ring[1], two), ring_pairs(2)))
    one_across = send(one[16:], across_pairs(False))
    two_across = send(two[16:], across_pairs(True))
    d_one = jnp.where(even, 0, 1)
    one = jnp.where(x_side == (col - d_one) % 16 // 8, one[:16], one_across)
    two = jnp.where(x_side == (col - 2) % 16 // 8, two[:16], two_across)
    moving = after(jnp.where(even, two, one), ring[1])
    ring.append(send(after(ring[2], moving), ring_pairs(3)))
    shifted = send(moving, shift_pairs())
    swapped_one = send(one, everyone(swap))
    small_once = one_back(after(small, swapped_one))
    shifted = after(shifted, big_once, swapped_one, small, ring[3])
    ring.append(send(after(ring[3], shifted), ring_pairs(4)))
    swapped = send(shifted, everyone(swap))
    first, swapped_first = one, swapped_one
    raw = jnp.concatenate(
        [
            jnp.where(even, first, swapped_first),
            jnp.where(even, swapped, shifted),
            jnp.where(even, shifted, swapped),
        ],
        axis=0,
    )
    half = [lax.dynamic_slice_in_dim(w_proj, 256 + 128 * v + 64 * core, 64, 1) for v in range(2)]
    mine = right_piece(raw, gain, bias, jnp.concatenate(half, axis=1).T)
    mine = after(mine, ring[4])
    ring.append(send(after(ring[4], mine), ring_pairs(5)))
    got = {0: mine}

    def exchange(value, n):
        return send(value, everyone(lambda r, c: (r ^ (2 * n), c)))

    swapped_mine = send(mine, everyone(swap))
    for n in (4, 1, 3):
        got[n] = exchange(mine, n)
    stage = after(got[4], got[1], got[3], small_once, ring[5])
    ring.append(send(after(ring[5], stage), ring_pairs(6)))
    got[5], got[7] = exchange(stage, 1), exchange(stage, 3)
    got[2] = exchange(after(mine, stage), 2)
    big_twice = one_back(after(big_once, stage))
    stage = after(got[4], got[5], got[7], got[2], ring[6])
    ring.append(send(after(ring[6], stage), ring_pairs(7)))
    got[6] = exchange(stage, 2)
    small_twice = one_back(after(small_once, got[6]))
    rights = [mine, swapped_mine]
    for n in range(1, 8):
        rights += [got[n], send(got[n], everyone(swap))]

    where = jnp.stack([chip ^ (col // 2), core]).astype(jnp.int32)
    out_g = jnp.broadcast_to(out_gain[:, None], (128, 128))
    out_b = jnp.broadcast_to(out_bias[:, None], (128, 128))

    groups = [(big, big_once, big_twice, big_gate), (small, small_once, small_twice, small_gate)]
    groups.append((whirl, ring[7], ring[6], whirl_gate))
    return final(where, groups, rights, out_g, out_b, w_out, None, 0)


def solution(mesh):
    in_specs = (P("row", "col", None), P(), P(), P(), P(), P(), P(), P())
    out_specs = P("row", "col", None)
    return jax.shard_map(shards, mesh=mesh, in_specs=in_specs, out_specs=out_specs, check_vma=False)
```

```python
import functools

import jax
import jax.numpy as jnp
from jax import lax
from jax.experimental import pallas as pl
from jax.experimental.pallas import tpu as pltpu
from jax.sharding import PartitionSpec as P

EPSILON = 1e-05
F32, BF16 = jnp.float32, jnp.bfloat16
NT = (((1,), (1,)), ((), ()))
TN = (((0,), (0,)), ((), ()))
AXES = ("row", "col")
BIG, SMALL = (0, 112), (112, 16)


def place(r, c):
    return (r % 16) * 16 + c % 16


def everyone(move):
    return [(place(r, c), place(*move(r, c))) for r in range(16) for c in range(16)]


def side(row):
    return row % 16 // 8


def scatter_pairs(a):
    return [(place(c, c + d), place(c ^ (2 * a), c + d)) for c in range(16) for d in range(3)]


def across_pairs(third):
    pairs = []
    for r in range(16):
        for c in range(16):
            even = (r - c) % 2 == 0
            d = 2 if third else 0 if even else 1
            if (even or not third) and side(r) == side(c - d):
                pairs.append((place(r, c), place(r ^ 8, c)))
    return pairs


def shift_pairs():
    return everyone(lambda r, c: (r, c - 2) if (r - c) % 2 == 0 else (r ^ 1, c - 1))


def back(r, c):
    return (r, c - 1)


def swap(r, c):
    return (r ^ 1, c)


def after(value, *others):
    return lax.optimization_barrier((value,) + others)[0]


def send(value, pairs):
    return lax.ppermute(value, AXES, pairs)


def sigmoid(x):
    return 0.5 * jnp.tanh(0.5 * x) + 0.5


def normed_rows(x, gain, bias):
    mean_of = jnp.full((128, 128), 1 / 128, BF16)
    centred = x.astype(F32) - jnp.dot(x, mean_of, preferred_element_type=F32)
    square = centred * centred
    high = square.astype(BF16)
    low = (square - high.astype(F32)).astype(BF16)
    variance = jnp.dot(high, mean_of, preferred_element_type=F32) + jnp.dot(
        low, mean_of, preferred_element_type=F32
    )
    return (centred * lax.rsqrt(variance + EPSILON) * gain + bias).astype(BF16)


def left_kernel(x_ref, gain_ref, bias_ref, wt_ref, wg_ref, left_ref, gate_ref, scratch):
    n = normed_rows(x_ref[...].reshape(16 * 128, 128), gain_ref[...], bias_ref[...])
    gate_ref[...] = sigmoid(jnp.dot(n, wg_ref[...], preferred_element_type=F32)).reshape(16, 128, 128)
    p = lax.dot_general(wt_ref[...], n, NT, preferred_element_type=F32)
    v = sigmoid(p[:128]) * p[128:]
    for i in range(16):
        scratch[i * 136 : i * 136 + 128, :] = v[:, i * 128 : (i + 1) * 128]

    def turn(h, _):
        left_ref[h] = scratch[pl.ds(h, 16, stride=136), :].astype(BF16)
        return 0

    lax.fori_loop(0, 128, turn, 0, unroll=16)


def whole(a):
    return pl.BlockSpec(a.shape, lambda *_: (0,) * a.ndim)


def left_and_gate(pair, start, rows, gain, bias, wt, w_gate):
    first = start // 16
    return pl.pallas_call(
        left_kernel,
        out_shape=[
            jax.ShapeDtypeStruct((128, rows, 128), BF16),
            jax.ShapeDtypeStruct((rows, 128, 128), F32),
        ],
        grid=(rows // 16,),
        in_specs=[
            pl.BlockSpec((16, 128, 128), lambda i: (first + i, 0, 0)),
            whole(gain),
            whole(bias),
            whole(wt),
            whole(w_gate),
        ],
        out_specs=[
            pl.BlockSpec((128, 16, 128), lambda i: (0, i, 0)),
            pl.BlockSpec((16, 128, 128), lambda i: (i, 0, 0)),
        ],
        scratch_shapes=[pltpu.VMEM((16 * 136, 128), F32)],
        compiler_params=pltpu.CompilerParams(vmem_limit_bytes=48 << 20),
        cost_estimate=pl.CostEstimate(
            flops=rows * 128 * 128 * 2 * 768, bytes_accessed=rows * 128 * 128 * 8, transcendentals=rows * 128 * 256
        ),
    )(pair, gain, bias, wt, w_gate)


def right_kernel(x_ref, gain_ref, bias_ref, wt_ref, right_ref, scratch):
    d = pl.program_id(0)
    n = normed_rows(x_ref[...].reshape(16 * 128, 128), gain_ref[...], bias_ref[...])
    p = lax.dot_general(wt_ref[...], n, NT, preferred_element_type=F32)
    v = sigmoid(p[:64]) * p[64:]
    for j in range(16):
        scratch[j * 72 : j * 72 + 64, :] = v[:, j * 128 : (j + 1) * 128]

    def turn(h, _):
        right_ref[h] = scratch[pl.ds(h, 16, stride=72), :].astype(BF16)
        return 0

    lax.fori_loop(0, 64, turn, 0, unroll=16)


def right_piece(pieces, gain, bias, wt):
    return pl.pallas_call(
        right_kernel,
        out_shape=jax.ShapeDtypeStruct((64, 16, 384), BF16),
        grid=(3,),
        in_specs=[pl.BlockSpec((16, 128, 128), lambda d: (d, 0, 0)), whole(gain), whole(bias), whole(wt)],
        out_specs=pl.BlockSpec((64, 16, 128), lambda d: (0, 0, d)),
        scratch_shapes=[pltpu.VMEM((16 * 72, 128), F32)],
        compiler_params=pltpu.CompilerParams(vmem_limit_bytes=32 << 20),
        cost_estimate=pl.CostEstimate(flops=48 * 128 * 128 * 2 * 384, bytes_accessed=3 << 20, transcendentals=48 * 128 * 64),
    )(pieces, gain, bias, wt)


STEP = 8


def final_kernel(place_ref, *refs, subs, aliased):
    count = len(subs)
    lefts = [refs[4 * s : 4 * s + 3] for s in range(count)]
    gates = [refs[4 * s + 3] for s in range(count)]
    rest = refs[4 * count :]
    rights, rest = rest[:16], rest[16:]
    gain_ref, bias_ref, w_ref = rest[:3]
    out_ref, scratch = rest[3 + aliased :]
    rows = sum(subs)
    step = pl.program_id(0)
    block, core = place_ref[0], place_ref[1]
    for half in range(2):
        which = core if half == 0 else 1 - core
        for t in range(STEP):
            left = jnp.concatenate(
                [jnp.concatenate([ref[which, t] for ref in sub], axis=-1) for sub in lefts], axis=0
            )
            right = jnp.concatenate([rights[2 * n + half][t] for n in range(8)], axis=0)
            h = which * 64 + step * STEP + t
            scratch[pl.ds(h * (rows + 1), rows), :] = lax.dot_general(
                left, right, NT, preferred_element_type=F32
            )

    @pl.when(step == 64 // STEP - 1)
    def _():
        base = 0
        for sub, gate_ref in zip(subs, gates):

            def some_rows(q, _, base=base, gate_ref=gate_ref):
                parts = []
                for e in range(16):
                    x = scratch[pl.ds(base + q * 16 + e, 128, stride=rows + 1), :]
                    centred = x - jnp.mean(x, axis=0, keepdims=True)
                    variance = jnp.mean(centred * centred, axis=0, keepdims=True)
                    parts.append(
                        (centred * lax.rsqrt(variance + EPSILON) * gain_ref[...] + bias_ref[...]).astype(BF16)
                    )
                y = jnp.concatenate(parts, axis=1)
                out = lax.dot_general(y, w_ref[...], TN, preferred_element_type=F32)
                for e in range(16):
                    for n in range(8):
                        chip = block ^ n
                        at = pl.ds(pl.multiple_of(chip % 4 * 32 + chip // 4 * 16, 16), 16)
                        mine = out[e * 128 + n * 16 : e * 128 + n * 16 + 16]
                        out_ref[base + q * 16 + e, at, :] = (gate_ref[q * 16 + e, at, :] * mine).astype(BF16)
                return 0

            lax.fori_loop(0, sub // 16, some_rows, 0)
            base += sub


def final(where, groups, rights, gain, bias, w_out, update, block):
    subs = tuple(g[3].shape[0] for g in groups)
    rows = sum(subs)
    operands, specs = [], []
    for l0, l1, l2, gate in groups:
        for l in (l0, l1, l2):
            operands.append(l.reshape(2, 64, gate.shape[0], 128))
            specs.append(pl.BlockSpec((2, STEP, gate.shape[0], 128), lambda s, _: (0, s, 0, 0)))
        operands.append(gate)
        specs.append(whole(gate))
    operands += rights
    specs += [pl.BlockSpec((STEP, 16, 384), lambda s, _: (s, 0, 0))] * 16
    operands += [gain, bias, w_out]
    specs += [whole(gain), whole(bias), whole(w_out)]
    aliases = {}
    if update is not None:
        aliases = {1 + len(operands): 0}
        operands.append(update)
        specs.append(pl.BlockSpec(memory_space=pl.ANY))
    return pl.pallas_call(
        functools.partial(final_kernel, subs=subs, aliased=len(aliases)),
        out_shape=jax.ShapeDtypeStruct((128, 128, 128), BF16),
        grid_spec=pltpu.PrefetchScalarGridSpec(
            num_scalar_prefetch=1,
            grid=(64 // STEP,),
            in_specs=specs,
            out_specs=pl.BlockSpec((rows, 128, 128), lambda s, _: (block, 0, 0)),
            scratch_shapes=[pltpu.VMEM((128 * (rows + 1), 128), F32)],
        ),
        input_output_aliases=aliases,
        compiler_params=pltpu.CompilerParams(vmem_limit_bytes=56 << 20),
        cost_estimate=pl.CostEstimate(
            flops=rows * 128 * 128 * 2 * 512, bytes_accessed=(14 << 20) + rows * 128 * 128 * 12, transcendentals=0
        ),
    )(where, *operands)


def shards(pair, ln_gain, ln_bias, w_proj, w_gate, out_gain, out_bias, w_out):
    row, col = lax.axis_index("row"), lax.axis_index("col")
    core, chip = row % 2, row // 2
    gain, bias = ln_gain[None, :], ln_bias[None, :]

    wt_left = w_proj[:, :256].T

    def left_of(part, source):
        return left_and_gate(source, *part, gain, bias, wt_left, w_gate)

    def one_back(value):
        return send(value, everyone(back))

    quarters = [pair[:32]] + [send(pair[32 * a : 32 * a + 32], scatter_pairs(a)) for a in (1, 2, 3)]
    big, big_gate = left_of(BIG, pair)
    big_once = one_back(big)
    small, small_gate = left_of(SMALL, pair)
    quarters[1] = after(quarters[1], big, small)
    even = core == col % 2
    y, x_side = chip % 4, chip // 4

    def quarter_of(d):
        away = y ^ ((col - d) % 16 // 2 % 4)
        picked = quarters[0]
        for a in range(1, 4):
            picked = jnp.where(away == a, quarters[a], picked)
        return picked

    one = jnp.where(even, quarter_of(0), quarter_of(1))
    two = quarter_of(2)
    one_across = send(one[16:], across_pairs(False))
    two_across = send(two[16:], across_pairs(True))
    d_one = jnp.where(even, 0, 1)
    one = jnp.where(x_side == (col - d_one) % 16 // 8, one[:16], one_across)
    two = jnp.where(x_side == (col - 2) % 16 // 8, two[:16], two_across)
    moving = jnp.where(even, two, one)
    shifted = send(moving, shift_pairs())
    swapped_one = send(one, everyone(swap))
    small_once = one_back(after(small, swapped_one))
    shifted = after(shifted, big_once, swapped_one, small)
    swapped = send(shifted, everyone(swap))
    first, swapped_first = one, swapped_one
    raw = jnp.concatenate(
        [
            jnp.where(even, first, swapped_first),
            jnp.where(even, swapped, shifted),
            jnp.where(even, shifted, swapped),
        ],
        axis=0,
    )
    half = [lax.dynamic_slice_in_dim(w_proj, 256 + 128 * v + 64 * core, 64, 1) for v in range(2)]
    mine = right_piece(raw, gain, bias, jnp.concatenate(half, axis=1).T)
    got = {0: mine}

    def exchange(value, n):
        return send(value, everyone(lambda r, c: (r ^ (2 * n), c)))

    swapped_mine = send(mine, everyone(swap))
    for n in (4, 1, 3):
        got[n] = exchange(mine, n)
    stage = after(got[4], got[1], got[3], small_once)
    got[5], got[7] = exchange(stage, 1), exchange(stage, 3)
    got[2] = exchange(after(mine, stage), 2)
    big_twice = one_back(after(big_once, stage))
    stage = after(got[4], got[5], got[7], got[2])
    got[6] = exchange(stage, 2)
    small_twice = one_back(after(small_once, got[6]))
    rights = [mine, swapped_mine]
    for n in range(1, 8):
        rights += [got[n], send(got[n], everyone(swap))]

    where = jnp.stack([chip ^ (col // 2), core]).astype(jnp.int32)
    out_g = jnp.broadcast_to(out_gain[:, None], (128, 128))
    out_b = jnp.broadcast_to(out_bias[:, None], (128, 128))

    groups = [(big, big_once, big_twice, big_gate), (small, small_once, small_twice, small_gate)]
    return final(where, groups, rights, out_g, out_b, w_out, None, 0)


def solution(mesh):
    in_specs = (P("row", "col", None), P(), P(), P(), P(), P(), P(), P())
    out_specs = P("row", "col", None)
    return jax.shard_map(shards, mesh=mesh, in_specs=in_specs, out_specs=out_specs, check_vma=False)
```
